128 devices in a mesh: gx: 16 (over y, z), gy: 8 (over x, core).
Axes of the slice: x: 4, y: 4, z: 4, core: 2. Of those that a mesh axis runs over, the one named last changes fastest.
Arguments:
- features: bfloat16 [48, 64, 32, 128], P(None, 'gx', 'gy'), may hold values from -6 to 6
- conv_one: bfloat16 [3, 3, 3, 1152], replicated, may hold values from -0.25 to 0.25
- conv_two: bfloat16 [3, 3, 3, 1152], replicated, may hold values from -0.25 to 0.25
- down_weight: bfloat16 [2, 2, 2, 4608], replicated, may hold values from -0.3125 to 0.3125
- coarse_weight: bfloat16 [3, 3, 3, 18432], replicated, may hold values from -0.125 to 0.125
- cotangent: float32 [192, 32, 1024], P('gx', None, 'gy'), may hold values from -6 to 6
Outputs:
- coarse_out: bfloat16 [192, 32, 1024], P('gx', None, 'gy')
- grad_input: bfloat16 [48, 64, 32, 128], P(None, 'gx', 'gy')
- grad_one: float32 [3, 3, 3, 1152], replicated
- grad_two: float32 [3, 3, 3, 1152], replicated
- grad_down: float32 [2, 2, 2, 4608], replicated
- grad_coarse: float32 [3, 3, 3, 18432], replicated
The draws below stay inside these ranges and needn't reach their ends.
All inputs are finite; a program needn't handle non-finite values.
Results may differ from the reference program's by a relative error of at most 0.02.
Values may be sent and summed in bfloat16 or wider, within the bound.
No kernel may reach another device: no remote copies, remote signals or barrier semaphores. Data moves between devices by JAX's collectives and lax.ppermute only.
A program may use at most 128 MiB of HBM per device.

```python
import jax
import jax.numpy as jnp
from jax import lax

C = 48
GROUPS = 2
CD = 96
CC = 192
KERN = 3
NZ = 128
NX = 64
NY = 32


def levels(key, shape, split, smallest, largest):
    gain, own = 1.0, jax.random.fold_in(key, 6)
    for position, shards_of in split:
        draws = jnp.exp(jax.random.uniform(jax.random.fold_in(own, position), (shards_of,), jnp.float32, smallest / len(split), largest / len(split)))
        gain = gain * jnp.repeat(draws, shape[position] // shards_of).reshape([-1 if axis == position else 1 for axis in range(len(shape))])
    return gain


def normal_values(own_key, dims, deviation, bound, pieces=(), held_as=jnp.bfloat16):
    gain = levels(own_key, dims, pieces, -0.22, 0.18) if pieces else 1.0
    array = jax.random.normal(own_key, dims, jnp.float32) * deviation * gain
    return jnp.minimum(jnp.maximum(array, -bound), bound).astype(held_as)


def setup_inputs(seed: int = 0) -> dict:
    key_of = jax.random.split(jax.random.key(seed), 7)
    features = normal_values(key_of[0], (C, NX, NY, NZ), 1.0, 6.0, ((1, 16), (2, 8)))
    conv_one = normal_values(key_of[1], (KERN, KERN, KERN, C * (C // GROUPS)), (C // GROUPS * 27) ** -0.5, 0.25)
    conv_two = normal_values(key_of[2], (KERN, KERN, KERN, C * (C // GROUPS)), (C // GROUPS * 27) ** -0.5, 0.25)
    down_weight = normal_values(key_of[3], (2, 2, 2, CD * C), (C * 8) ** -0.5, 0.3125)
    coarse_weight = normal_values(key_of[4], (KERN, KERN, KERN, CC * CD), (CD * 27) ** -0.5, 0.125)
    cotangent = normal_values(key_of[5], (CC, NX // 2, (NY // 2) * (NZ // 2)), 1.0, 6.0, ((0, 16), (2, 8)), jnp.float32)
    return {"features": features, "conv_one": conv_one, "conv_two": conv_two, "down_weight": down_weight, "coarse_weight": coarse_weight, "cotangent": cotangent}


def as_kernel(flat, outer):
    extent = flat.shape[0]
    inner = flat.shape[3] // outer
    return jnp.transpose(flat.reshape(extent, extent, extent, outer, inner), (3, 4, 0, 1, 2))

def as_flat(kernel):
    outer, inner, extent = (kernel.shape[0], kernel.shape[1], kernel.shape[2])
    return jnp.transpose(kernel, (2, 3, 4, 0, 1)).reshape(extent, extent, extent, outer * inner)

def conv_same(field, kernel, groups):
    return lax.conv_general_dilated(field.astype(jnp.float32)[None], kernel.astype(jnp.float32), (1, 1, 1), 'SAME', dimension_numbers=('NCDHW', 'OIDHW', 'NCDHW'), feature_group_count=groups, precision=lax.Precision.HIGHEST)[0]

def shrink_same(field, kernel):
    return lax.conv_general_dilated(field.astype(jnp.float32)[None], kernel.astype(jnp.float32), (2, 2, 2), 'VALID', dimension_numbers=('NCDHW', 'OIDHW', 'NCDHW'), precision=lax.Precision.HIGHEST)[0]

def slope(value):
    sig = jax.nn.sigmoid(value)
    return sig * (1.0 + value * (1.0 - sig))

def reference(features, conv_one, conv_two, down_weight, coarse_weight, cotangent):
    groups = GROUPS
    kernel_one = as_kernel(conv_one, C)
    kernel_two = as_kernel(conv_two, C)
    kernel_down = as_kernel(down_weight, CD)
    kernel_coarse = as_kernel(coarse_weight, CC)
    cot_cells = cotangent.reshape(CC, NX // 2, NY // 2, NZ // 2)
    pre_one, back_one = jax.vjp(lambda p, q: conv_same(p, q, groups), features.astype(jnp.float32), kernel_one.astype(jnp.float32))
    act_one = jax.nn.silu(pre_one).astype(jnp.bfloat16)
    pre_two, back_two = jax.vjp(lambda p, q: conv_same(p, q, groups), act_one.astype(jnp.float32), kernel_two.astype(jnp.float32))
    act_two = jax.nn.silu(pre_two).astype(jnp.bfloat16)
    coarse_f, back_down = jax.vjp(shrink_same, act_two.astype(jnp.float32), kernel_down.astype(jnp.float32))
    coarse_in = coarse_f.astype(jnp.bfloat16)
    pre_three, back_three = jax.vjp(lambda p, q: conv_same(p, q, 1), coarse_in.astype(jnp.float32), kernel_coarse.astype(jnp.float32))
    coarse_out = jax.nn.silu(pre_three).astype(jnp.bfloat16)
    grad_three = (cot_cells * slope(pre_three)).astype(jnp.bfloat16)
    coarse_grad, grad_coarse = back_three(grad_three.astype(jnp.float32))
    coarse_back = coarse_grad.astype(jnp.bfloat16)
    grad_act_two, grad_down = back_down(coarse_back.astype(jnp.float32))
    grad_mid_two = (grad_act_two * slope(pre_two)).astype(jnp.bfloat16)
    grad_act_one, grad_two = back_two(grad_mid_two.astype(jnp.float32))
    grad_mid_one = (grad_act_one * slope(pre_one)).astype(jnp.bfloat16)
    grad_feat, grad_one = back_one(grad_mid_one.astype(jnp.float32))
    merged_out = coarse_out.reshape(CC, NX // 2, NY // 2 * (NZ // 2))
    return (merged_out, grad_feat.astype(jnp.bfloat16), as_flat(grad_one), as_flat(grad_two), as_flat(grad_down), as_flat(grad_coarse))
```

```python
import jax
import jax.numpy as jnp
from jax import lax
from jax.experimental import pallas as pl
from jax.experimental.pallas import tpu as pltpu
from jax.sharding import PartitionSpec as P

BF = jnp.bfloat16
F32 = jnp.float32
C = 48
CD = 96
CC = 192
Z = 128
ALL = ("gx", "gy")
VMEM_LIMIT = 24 * 1024 * 1024


def dot(a, b):
    return jnp.dot(a, b, preferred_element_type=F32)


def dot_t(a, b):
    return lax.dot_general(a, b, (((1,), (1,)), ((), ())), preferred_element_type=F32)


def sigmoid(v):
    return 0.5 * jnp.tanh(0.5 * v) + 0.5


def from_before(v, segment):
    lane = lax.broadcasted_iota(jnp.int32, v.shape, 1)
    return jnp.where(lane % segment == 0, 0.0, pltpu.roll(v, 1, 1))


def from_after(v, segment):
    lane = lax.broadcasted_iota(jnp.int32, v.shape, 1)
    return jnp.where(lane % segment == segment - 1, 0.0, pltpu.roll(v, Z - 1, 1))


def tap_sum(y, lanes, rows, segment, flipped):
    one, two, three = (y[k * rows : (k + 1) * rows, lanes * Z : (lanes + 1) * Z] for k in range(3))
    if flipped:
        return from_after(one, segment) + two + from_before(three, segment)
    return from_before(one, segment) + two + from_after(three, segment)


def swap_halves(v):
    return pltpu.roll(v.astype(F32), Z // 2, 1)


def low_lanes(shape):
    return lax.broadcasted_iota(jnp.int32, shape, 1) < Z // 2


def fine_kernel(
    flags, feat_l, feat_m, feat_r, w_one, w_two, w_down,
    act_one, slope_one, slope_two, down_own, coarse_in,
    stack, field, rows_two, down_all,
):
    feats = (feat_l, feat_m, feat_r)

    def valid(x, lo, hi):
        ok_l = jnp.where(x < lo, flags[0], 1.0)
        return jnp.where(x >= hi, flags[1], ok_l)

    def valid_y(y, lo, hi):
        if y < lo:
            return flags[2]
        if y >= hi:
            return flags[3]
        return 1.0

    def step_one(x, carry):
        for a in range(3):
            for y in range(12):
                piece = feats[y // 4][x + a, (y % 4) * C : (y % 4 + 1) * C, :]
                for b in range(3):
                    if 0 <= y - b < 10:
                        stack[(a * 3 + b) * C : (a * 3 + b + 1) * C, (y - b) * Z : (y - b + 1) * Z] = piece
        prod = dot(w_one[...], stack[...])
        ok_x = valid(x, 3, 7)
        for y in range(10):
            pre = tap_sum(prod, y, C, Z, False)
            sig = sigmoid(pre)
            ok = ok_x * valid_y(y, 3, 7)
            act = (pre * sig * ok).astype(BF)
            field[x, y * C : (y + 1) * C, :] = act
            if 2 <= y < 8:
                slp = sig * (1.0 + pre * (1.0 - sig)) * ok

                @pl.when(jnp.logical_and(x >= 2, x < 8))
                def _():
                    act_one[x - 2, (y - 2) * C : (y - 1) * C, :] = act
                    slope_one[x - 2, (y - 2) * C : (y - 1) * C, :] = slp

        return carry

    lax.fori_loop(0, 10, step_one, 0)

    row = lax.broadcasted_iota(jnp.int32, (2 * Z, 2 * Z), 0)
    col = lax.broadcasted_iota(jnp.int32, (2 * Z, 2 * Z), 1)
    same = (row // Z) == (col % Z) // (Z // 2)
    select = jnp.where(same & (row % Z == 2 * (col % (Z // 2)) + col // Z), 1.0, 0.0).astype(BF)

    def step_two(x, carry):
        for a in range(3):
            for y in range(10):
                piece = field[x + a, y * C : (y + 1) * C, :]
                for b in range(3):
                    if 0 <= y - b < 8:
                        stack[(a * 3 + b) * C : (a * 3 + b + 1) * C, (y - b) * Z : (y - b + 1) * Z] = piece
        prod = dot(w_two[...], stack[:, : 8 * Z])
        ok_x = valid(x, 2, 6)
        for y in range(8):
            pre = tap_sum(prod, y, C, Z, False)
            sig = sigmoid(pre)
            ok = ok_x * valid_y(y, 2, 6)
            act = (pre * sig * ok).astype(BF)
            slope_two[x, y * C : (y + 1) * C, :] = sig * (1.0 + pre * (1.0 - sig)) * ok
            pair, b = y // 2, y % 2
            if pair < 3:
                rows_two[(pair * 2 + b) * C : (pair * 2 + b + 1) * C, :Z] = act
            if pair > 0:
                rows_two[((pair - 1) * 2 + b) * C : ((pair - 1) * 2 + b + 1) * C, Z:] = act
        picked = dot(rows_two[...], select).astype(BF)
        a = x % 2
        for pair in range(3):
            for b in range(2):
                for c in range(2):
                    at = pl.multiple_of(a * (4 * C) + (b * 2 + c) * C, 16)
                    down_all[x // 2, pl.ds(at, C), pair * Z : (pair + 1) * Z] = picked[
                        (pair * 2 + b) * C : (pair * 2 + b + 1) * C, c * Z : (c + 1) * Z
                    ]
        return carry

    lax.fori_loop(0, 8, step_two, 0)

    for x in range(2):
        down_own[x] = down_all[x + 1, :, Z : 2 * Z]
    for x in range(4):
        coarse_in[x] = dot(w_down[...], down_all[x]).astype(BF)


def coarse_kernel(coarse_in, w_coarse, cot, coarse_out, grad_three):
    total = jnp.zeros((3 * CC, 2 * Z), F32)
    for a in range(3):
        for b in range(3):
            cells = jnp.concatenate(
                [coarse_in[a + x, :, b * Z : (b + 1) * Z] for x in range(2)], axis=1
            )
            total = total + dot(w_coarse[a * 3 + b], cells)
    for x in range(2):
        pre = tap_sum(total, x, CC, Z // 2, False)
        sig = sigmoid(pre)
        coarse_out[x] = (pre * sig).astype(BF)
        grad_three[x] = (cot[x].astype(F32) * (sig * (1.0 + pre * (1.0 - sig)))).astype(BF)


def grouped(taps, c):
    first = lax.broadcasted_iota(jnp.int32, (C, C // 2), 0) < C // 2
    parts = []
    for ab in range(9):
        tap = taps[ab * 3 + c].astype(F32)
        parts += [jnp.where(first, tap, 0.0), jnp.where(first, 0.0, tap)]
    return jnp.concatenate(parts, axis=1)


def ahead_kernel(one, two, down, w_one, w_two, w_down):
    for taps, out in ((one, w_one), (two, w_two)):
        for c in range(3):
            out[c * C : (c + 1) * C, :] = grouped(taps, c).astype(BF)
    w_down[...] = jnp.concatenate([down[k].astype(F32) for k in range(8)], axis=1).astype(BF)


def back_kernel(one, two, down, coarse, w_one_t, w_two_t, w_down_t, w_coarse_t):
    for taps, out in ((one, w_one_t), (two, w_two_t)):
        for c in range(3):
            turned = grouped(taps, c).T
            out[c * C : (c + 1) * C, :] = jnp.concatenate(
                [turned[ab * C : (ab + 1) * C, :] for ab in range(9)], axis=1
            ).astype(BF)
    for ab in range(4):
        w_down_t[ab * C : (ab + 1) * C, :] = jnp.concatenate(
            [down[ab * 2 + c].astype(F32).T for c in range(2)], axis=1
        ).astype(BF)

    def turn(ab, carry):
        for c in range(3):
            w_coarse_t[ab, c * CD : (c + 1) * CD, :] = (
                coarse[ab, c * CC : (c + 1) * CC, :].astype(F32).T.astype(BF)
            )
        return carry

    lax.fori_loop(0, 9, turn, 0)


def final_kernel(rows, out, wide):
    wide[...] = rows[...].astype(F32)
    for ab in range(9):
        for r in range(144):
            q, s = r // 3, r % 3
            out[ab // 3, ab % 3, :, r * Z : (r + 1) * Z] = wide[
                pl.ds(ab * 432 + s * 48 + q, 3, stride=144), :
            ]


def coarse_grad_kernel(grad_three, coarse_in, out, shifted, left):
    for x in range(2):
        grad = grad_three[x].astype(F32)
        lanes = slice(x * Z, (x + 1) * Z)
        shifted[x, 0] = from_after(grad, Z // 2)
        shifted[x, 1] = grad
        shifted[x, 2] = from_before(grad, Z // 2)
        for c in range(3):
            for r in range(4):
                left[(c * 4 + r) * 48 : (c * 4 + r + 1) * 48, lanes] = shifted[
                    x, c, pl.ds(r, 48, stride=4), :
                ].astype(BF)
    for a in range(3):
        for b in range(3):
            cells = jnp.concatenate(
                [coarse_in[a + x, :, b * Z : (b + 1) * Z] for x in range(2)], axis=1
            )
            part = dot_t(left[...], cells)
            for c in range(3):
                wide = jnp.concatenate(
                    [part[(c * 4 + r) * 48 : (c * 4 + r + 1) * 48, :] for r in range(4)], axis=1
                ).astype(BF)
                tap = (a * 3 + b) * 3 + c
                for s in range(3):
                    at = (tap * 3 + s) * 48
                    out[at : at + 48, :] = wide[:, s * Z : (s + 1) * Z]
    out[81 * 48 :, :] = jnp.zeros((4096 - 81 * 48, Z), BF)


def backward_kernel(
    g_l, g_m, g_r, feat_l, feat_m, feat_r, act_one, slope_one, slope_two, down_own,
    w_one_t, w_two_t, w_down_t, w_coarse_t,
    grad_input, small,
    halves, spread, mid_two, mid_one, stack, left,
):
    low = low_lanes((CC, Z))

    def prepare(x, carry):
        p0, p1, p2 = g_l[x], g_m[x], g_r[x]
        s0, s1, s2 = swap_halves(p0), swap_halves(p1), swap_halves(p2)
        halves[0, x, :, :Z] = p1
        halves[0, x, :, Z:] = p2
        halves[1, x, :, :Z] = jnp.where(low, s0, s1).astype(BF)
        halves[1, x, :, Z:] = jnp.where(low, s1, s2).astype(BF)
        halves[2, x, :, :Z] = p0
        halves[2, x, :, Z:] = p1
        return carry

    lax.fori_loop(0, 6, prepare, 0)

    row = lax.broadcasted_iota(jnp.int32, (Z, 4 * Z), 0)
    col = lax.broadcasted_iota(jnp.int32, (Z, 4 * Z), 1)
    same = row // (Z // 2) == col // (2 * Z)
    place = jnp.where(same & (col % Z == 2 * (row % (Z // 2)) + (col // Z) % 2), 1.0, 0.0).astype(BF)
    low_down = low_lanes((CD, Z))

    grad_down = jnp.zeros((CD, 8 * C), F32)
    for x in range(4):
        total = jnp.zeros((3 * CD, 2 * Z), F32)
        for a in range(3):
            for b in range(3):
                total = total + dot(w_coarse_t[a * 3 + b], halves[b, x + 2 - a])
        back = [tap_sum(total, k, CD, Z // 2, True).astype(BF) for k in range(2)]
        if x == 1 or x == 2:
            own = jnp.where(low_down, swap_halves(back[0]), swap_halves(back[1])).astype(BF)
            grad_down = grad_down + dot_t(own, down_own[x - 1])
        for k in range(2):
            wide = dot(back[k], place).astype(BF)
            for y in range(2):
                for c in range(2):
                    spread[c * CD : (c + 1) * CD, (k * 2 + y) * Z : (k * 2 + y + 1) * Z] = wide[
                        :, (y * 2 + c) * Z : (y * 2 + c + 1) * Z
                    ]
        fine = dot(w_down_t[...], spread[...])
        for a in range(2):
            for b in range(2):
                for y in range(4):
                    rows = slice((2 * y + b) * C, (2 * y + b + 1) * C)
                    part = fine[(a * 2 + b) * C : (a * 2 + b + 1) * C, y * Z : (y + 1) * Z]
                    mid_two[2 * x + a, rows, :] = (part * slope_two[2 * x + a, rows, :]).astype(BF)
    for s in range(3):
        small[1152 + s * CD : 1152 + (s + 1) * CD, :] = grad_down[:, s * Z : (s + 1) * Z].astype(BF)

    def kernel_grad(grad_of, field_of, at):
        for x in range(4):
            for y in range(4):
                lanes = slice((x * 4 + y) * Z, (x * 4 + y + 1) * Z)
                grad = grad_of(x, y).astype(F32)
                left[:C, lanes] = from_after(grad, Z).astype(BF)
                left[C : 2 * C, lanes] = grad.astype(BF)
                left[2 * C :, lanes] = from_before(grad, Z).astype(BF)
        for x in range(6):
            for y in range(6):
                piece = field_of(x, y)
                for a in range(3):
                    for b in range(3):
                        if 0 <= x - a < 4 and 0 <= y - b < 4:
                            cell = (x - a) * 4 + (y - b)
                            stack[(a * 3 + b) * C : (a * 3 + b + 1) * C, cell * Z : (cell + 1) * Z] = piece
        part = dot_t(left[...], stack[...]).astype(BF)
        for s in range(3):
            small[at + s * 144 : at + (s + 1) * 144, :] = part[:, s * Z : (s + 1) * Z]
        small[at + 432 : at + 576, :48] = part[:, 3 * Z :]
        small[at + 432 : at + 576, 48:] = jnp.zeros((144, Z - 48), BF)

    kernel_grad(
        lambda x, y: mid_two[x + 2, (y + 2) * C : (y + 3) * C, :],
        lambda x, y: act_one[x, y * C : (y + 1) * C, :],
        576,
    )

    def step_two(x, carry):
        for a in range(3):
            for y in range(8):
                piece = mid_two[x + 2 - a, y * C : (y + 1) * C, :]
                for b in range(3):
                    at = y - 2 + b
                    if 0 <= at < 6:
                        stack[(a * 3 + b) * C : (a * 3 + b + 1) * C, at * Z : (at + 1) * Z] = piece
        prod = dot(w_two_t[...], stack[:, : 6 * Z])
        for y in range(6):
            rows = slice(y * C, (y + 1) * C)
            grad = tap_sum(prod, y, C, Z, True)
            mid_one[x, rows, :] = (grad * slope_one[x, rows, :]).astype(BF)
        return carry

    lax.fori_loop(0, 6, step_two, 0)

    feats = {-1: feat_l, 0: feat_m, 1: feat_r}

    def feature(x, y):
        fine_y = y - 1
        block = fine_y // 4
        return feats[block][x + 3, (fine_y % 4) * C : (fine_y % 4 + 1) * C, :]

    kernel_grad(lambda x, y: mid_one[x + 1, (y + 1) * C : (y + 2) * C, :], feature, 0)

    def step_one(x, carry):
        for a in range(3):
            for y in range(6):
                piece = mid_one[x + 2 - a, y * C : (y + 1) * C, :]
                for b in range(3):
                    at = y - 2 + b
                    if 0 <= at < 4:
                        stack[(a * 3 + b) * C : (a * 3 + b + 1) * C, at * Z : (at + 1) * Z] = piece
        prod = dot(w_one_t[...], stack[:, : 4 * Z])
        for y in range(4):
            grad_input[x, y * C : (y + 1) * C, :] = tap_sum(prod, y, C, Z, True).astype(BF)
        return carry

    lax.fori_loop(0, 4, step_one, 0)


def call(kernel, outs, scratch, n_smem, flops, *args):
    vmem = pl.BlockSpec(memory_space=pltpu.VMEM)
    smem = pl.BlockSpec(memory_space=pltpu.SMEM)
    moved = sum(a.size * a.dtype.itemsize for a in args) + sum(
        o.size * o.dtype.itemsize for o in outs
    )
    return pl.pallas_call(
        kernel,
        out_shape=outs,
        in_specs=[smem] * n_smem + [vmem] * (len(args) - n_smem),
        out_specs=[vmem] * len(outs),
        scratch_shapes=scratch,
        compiler_params=pltpu.CompilerParams(vmem_limit_bytes=VMEM_LIMIT),
        cost_estimate=pl.CostEstimate(flops=flops, bytes_accessed=moved, transcendentals=0),
    )(*args)


def shape(dims, dtype=BF):
    return jax.ShapeDtypeStruct(dims, dtype)


def neighbours(array, axis):
    size = lax.axis_size(axis)
    up = [(i, i + 1) for i in range(size - 1)]
    down = [(j, i) for i, j in up]
    return lax.ppermute(array, axis, up), lax.ppermute(array, axis, down)


def shares(parts):
    devices = lax.axis_size("gx") * lax.axis_size("gy")
    rows = parts.shape[0] // devices
    got = lax.all_to_all(parts.reshape(devices, rows, Z), ALL, 0, 0, tiled=True)
    return jnp.sum(got.astype(F32), axis=0).astype(BF)


def gathered(mine):
    devices = lax.axis_size("gx") * lax.axis_size("gy")
    spread = jnp.broadcast_to(mine[None], (devices,) + mine.shape)
    return lax.all_to_all(spread, ALL, 0, 0, tiled=True)


def fine_grad(rows):
    part = jnp.transpose(rows.reshape(4, 144, Z), (1, 0, 2)).reshape(144, 512)[:, :432]
    part = part.reshape(3, 2, 24, 3, 3, 2, 24)
    own = jnp.stack([part[:, g, :, :, :, g, :] for g in range(2)], axis=1)
    return jnp.transpose(own, (3, 4, 0, 1, 2, 5)).reshape(3, 3, 3, 1152).astype(F32)


def per_device(features, conv_one, conv_two, down_weight, coarse_weight, cotangent):
    gx, gy = lax.axis_index("gx"), lax.axis_index("gy")
    last_x, last_y = lax.axis_size("gx") - 1, lax.axis_size("gy") - 1
    flags = jnp.stack([gx > 0, gx < last_x, gy > 0, gy < last_y]).astype(F32)

    feat = jnp.transpose(features, (1, 2, 0, 3)).reshape(4, 4 * C, Z)
    before, after = neighbours(feat, "gx")
    feat = jnp.concatenate([before, feat, after], axis=0)
    feat, cot = lax.optimization_barrier((feat, cotangent.astype(BF)))
    feat_l, feat_r = neighbours(feat, "gy")

    cot = lax.all_to_all(
        cot.reshape(12, 16, 2, Z), "gx", split_axis=1, concat_axis=0, tiled=True
    )
    cot = jnp.transpose(cot.reshape(CC, 2, Z), (1, 0, 2))

    one = conv_one.reshape(27, C, C // 2)
    two = conv_two.reshape(27, C, C // 2)
    down = down_weight.reshape(8, CD, C)
    w_coarse = coarse_weight.reshape(9, 3 * CC, CD)
    w_one, w_two, w_down = call(
        ahead_kernel, [shape((144, 432)), shape((144, 432)), shape((CD, 8 * C))], [], 0, 0,
        one, two, down,
    )

    act_one, slope_one, slope_two, down_own, coarse_in = call(
        fine_kernel,
        [
            shape((6, 6 * C, Z)), shape((6, 6 * C, Z), F32), shape((8, 8 * C, Z), F32),
            shape((2, 8 * C, Z)), shape((4, CD, 3 * Z)),
        ],
        [
            pltpu.VMEM((9 * C, 10 * Z), BF), pltpu.VMEM((10, 10 * C, Z), BF),
            pltpu.VMEM((6 * C, 2 * Z), BF), pltpu.VMEM((4, 8 * C, 3 * Z), BF),
        ],
        1, 16_000_000_000,
        flags, feat_l, feat, feat_r, w_one, w_two, w_down,
    )
    coarse_out, grad_three = call(
        coarse_kernel, [shape((2, CC, Z)), shape((2, CC, Z))], [], 0, 300_000_000,
        coarse_in, w_coarse, cot,
    )

    before, after = neighbours(grad_three, "gx")
    one, two, down, coarse_t, grad_three = lax.optimization_barrier(
        (one, two, down, w_coarse, grad_three)
    )
    w_one_t, w_two_t, w_down_t, w_coarse_t = call(
        back_kernel,
        [shape((144, 432)), shape((144, 432)), shape((4 * C, 2 * CD)), shape((9, 3 * CD, CC))],
        [], 0, 0, one, two, down, coarse_t,
    )
    (coarse_part,) = call(
        coarse_grad_kernel,
        [shape((4096, Z))],
        [pltpu.VMEM((2, 3, CC, Z), F32), pltpu.VMEM((3 * CC, 2 * Z), BF)],
        0, 500_000_000,
        grad_three, coarse_in,
    )
    wide = jnp.concatenate([before, grad_three, after], axis=0)
    g_l, g_r = neighbours(wide, "gy")
    out = lax.all_to_all(
        coarse_out.reshape(2, 16, 12, Z), "gx", split_axis=1, concat_axis=0, tiled=True
    )
    g_l, g_r, coarse_part, out = lax.optimization_barrier((g_l, g_r, coarse_part, out))
    out = jnp.transpose(out.reshape(32, 12, Z), (1, 0, 2))
    coarse_mine = shares(coarse_part)

    grad_input, small = call(
        backward_kernel,
        [shape((4, 4 * C, Z)), shape((1536, Z))],
        [
            pltpu.VMEM((3, 6, CC, 2 * Z), BF), pltpu.VMEM((2 * CD, 4 * Z), BF),
            pltpu.VMEM((8, 8 * C, Z), BF), pltpu.VMEM((6, 6 * C, Z), BF),
            pltpu.VMEM((9 * C, 16 * Z), BF), pltpu.VMEM((144, 16 * Z), BF),
        ],
        0, 12_000_000_000,
        g_l, wide, g_r, feat_l, feat, feat_r, act_one, slope_one, slope_two, down_own,
        w_one_t, w_two_t, w_down_t, w_coarse_t,
    )
    small, coarse_mine = lax.optimization_barrier((small, coarse_mine))
    sums = gathered(jnp.concatenate([coarse_mine, shares(small)], axis=0))
    small_sum = sums[:, 32:].reshape(1536, Z)

    grad_input = jnp.transpose(grad_input.reshape(4, 4, C, Z), (2, 0, 1, 3))
    grad_one = fine_grad(small_sum[:576])
    grad_two = fine_grad(small_sum[576:1152])
    grad_down = jnp.transpose(
        small_sum[1152:1440].reshape(3, CD, Z), (1, 0, 2)
    ).reshape(CD, 8, C)
    grad_down = jnp.swapaxes(grad_down, 0, 1).reshape(2, 2, 2, CD * C).astype(F32)
    (grad_coarse,) = call(
        final_kernel, [shape((3, 3, 3, CC * CD), F32)], [pltpu.VMEM((4096, Z), F32)], 0, 0,
        sums[:, :32].reshape(4096, Z),
    )
    return out, grad_input, grad_one, grad_two, grad_down, grad_coarse


def solution(mesh):
    placed = (P(None, "gx", "gy", None), P(), P(), P(), P(), P("gx", None, "gy"))
    return jax.shard_map(
        per_device,
        mesh=mesh,
        in_specs=placed,
        out_specs=(P("gx", None, "gy"), P(None, "gx", "gy", None), P(), P(), P(), P()),
        check_vma=False,
    )
```

```python
import jax
import jax.numpy as jnp
from jax import lax
from jax.experimental import pallas as pl
from jax.experimental.pallas import tpu as pltpu
from jax.sharding import PartitionSpec as P

BF = jnp.bfloat16
F32 = jnp.float32
C = 48
CD = 96
CC = 192
Z = 128
GY = ("x", "core")
ALL = ("gx", "x", "core")
SAME_CORE = ("gx", "x")


def dot(a, b):
    return jnp.dot(a, b, preferred_element_type=F32)


def dot_t(a, b):
    return lax.dot_general(a, b, (((1,), (1,)), ((), ())), preferred_element_type=F32)


def sigmoid(v):
    return 0.5 * jnp.tanh(0.5 * v) + 0.5


def from_before(v, segment):
    lane = lax.broadcasted_iota(jnp.int32, v.shape, 1)
    return jnp.where(lane % segment == 0, 0.0, pltpu.roll(v, 1, 1))


def from_after(v, segment):
    lane = lax.broadcasted_iota(jnp.int32, v.shape, 1)
    return jnp.where(lane % segment == segment - 1, 0.0, pltpu.roll(v, Z - 1, 1))


def tap_sum(y, lanes, rows, segment, flipped):
    one, two, three = (y[k * rows : (k + 1) * rows, lanes * Z : (lanes + 1) * Z] for k in range(3))
    if flipped:
        return from_after(one, segment) + two + from_before(three, segment)
    return from_before(one, segment) + two + from_after(three, segment)


def swap_halves(v):
    return pltpu.roll(v.astype(F32), Z // 2, 1)


def low_lanes(shape):
    return lax.broadcasted_iota(jnp.int32, shape, 1) < Z // 2


def fine_kernel(
    flags, feat_l, feat_m, feat_r, one, two, down,
    kept_six, kept_eight, coarse_in,
    w_one, w_two, w_down, stack, field, rows_two, down_all, slope_a, slope_b, sems,
):
    feats = (feat_l, feat_m, feat_r)
    inner = pl.ds(3, 6)
    copies = [
        pltpu.make_async_copy(
            feat_l.at[inner, pl.ds(3 * C, C), :], kept_six.at[pl.ds(12, 6), pl.ds(0, C), :], sems.at[0]
        ),
        pltpu.make_async_copy(
            feat_m.at[inner], kept_six.at[pl.ds(12, 6), pl.ds(C, 4 * C), :], sems.at[1]
        ),
        pltpu.make_async_copy(
            feat_r.at[inner, pl.ds(0, C), :], kept_six.at[pl.ds(12, 6), pl.ds(5 * C, C), :], sems.at[2]
        ),
        pltpu.make_async_copy(
            field.at[pl.ds(2, 6), pl.ds(2 * C, 6 * C), :], kept_six.at[pl.ds(0, 6)], sems.at[3]
        ),
        pltpu.make_async_copy(slope_a, kept_six.at[pl.ds(6, 6)], sems.at[4]),
        pltpu.make_async_copy(slope_b, kept_eight.at[pl.ds(0, 8)], sems.at[5]),
        pltpu.make_async_copy(
            down_all.at[pl.ds(1, 2), :, pl.ds(Z, Z)], kept_eight.at[pl.ds(8, 2)], sems.at[6]
        ),
    ]
    for copy in copies[:3]:
        copy.start()
    for taps, w in ((one, w_one), (two, w_two)):
        for c in range(3):
            w[c * C : (c + 1) * C, :] = grouped(taps, c).astype(BF)
    w_down[...] = jnp.concatenate([down[k].astype(F32) for k in range(8)], axis=1).astype(BF)

    def valid(x, lo, hi):
        ok_l = jnp.where(x < lo, flags[0], 1.0)
        return jnp.where(x >= hi, flags[1], ok_l)

    def valid_y(y, lo, hi):
        if y < lo:
            return flags[2]
        if y >= hi:
            return flags[3]
        return 1.0

    def step_one(x, carry):
        for a in range(3):
            for y in range(12):
                piece = feats[y // 4][x + a, (y % 4) * C : (y % 4 + 1) * C, :]
                for b in range(3):
                    if 0 <= y - b < 10:
                        stack[(a * 3 + b) * C : (a * 3 + b + 1) * C, (y - b) * Z : (y - b + 1) * Z] = piece
        prod = dot(w_one[...], stack[...])
        ok_x = valid(x, 3, 7)
        for y in range(10):
            pre = tap_sum(prod, y, C, Z, False)
            sig = sigmoid(pre)
            ok = ok_x * valid_y(y, 3, 7)
            act = (pre * sig * ok).astype(BF)
            field[x, y * C : (y + 1) * C, :] = act
            if 2 <= y < 8:
                slp = (sig * (1.0 + pre * (1.0 - sig)) * ok).astype(BF)

                @pl.when(jnp.logical_and(x >= 2, x < 8))
                def _():
                    slope_a[x - 2, (y - 2) * C : (y - 1) * C, :] = slp

        return carry

    lax.fori_loop(0, 10, step_one, 0)
    copies[3].start()
    copies[4].start()

    row = lax.broadcasted_iota(jnp.int32, (2 * Z, 2 * Z), 0)
    col = lax.broadcasted_iota(jnp.int32, (2 * Z, 2 * Z), 1)
    same = (row // Z) == (col % Z) // (Z // 2)
    select = jnp.where(same & (row % Z == 2 * (col % (Z // 2)) + col // Z), 1.0, 0.0).astype(BF)

    def step_two(x, carry):
        for a in range(3):
            for y in range(10):
                piece = field[x + a, y * C : (y + 1) * C, :]
                for b in range(3):
                    if 0 <= y - b < 8:
                        stack[(a * 3 + b) * C : (a * 3 + b + 1) * C, (y - b) * Z : (y - b + 1) * Z] = piece
        prod = dot(w_two[...], stack[:, : 8 * Z])
        ok_x = valid(x, 2, 6)
        for y in range(8):
            pre = tap_sum(prod, y, C, Z, False)
            sig = sigmoid(pre)
            ok = ok_x * valid_y(y, 2, 6)
            act = (pre * sig * ok).astype(BF)
            slope_b[x, y * C : (y + 1) * C, :] = (sig * (1.0 + pre * (1.0 - sig)) * ok).astype(BF)
            pair, b = y // 2, y % 2
            if pair < 3:
                rows_two[(pair * 2 + b) * C : (pair * 2 + b + 1) * C, :Z] = act
            if pair > 0:
                rows_two[((pair - 1) * 2 + b) * C : ((pair - 1) * 2 + b + 1) * C, Z:] = act
        picked = dot(rows_two[...], select).astype(BF)
        a = x % 2
        for pair in range(3):
            for b in range(2):
                for c in range(2):
                    at = pl.multiple_of(a * (4 * C) + (b * 2 + c) * C, 16)
                    down_all[x // 2, pl.ds(at, C), pair * Z : (pair + 1) * Z] = picked[
                        (pair * 2 + b) * C : (pair * 2 + b + 1) * C, c * Z : (c + 1) * Z
                    ]
        return carry

    lax.fori_loop(0, 8, step_two, 0)
    copies[5].start()
    copies[6].start()
    for x in range(4):
        coarse_in[x] = dot(w_down[...], down_all[x]).astype(BF)
    for copy in copies:
        copy.wait()


def coarse_kernel(coarse_in, w_coarse, cot, coarse_out, grad_three):
    total = jnp.zeros((3 * CC, 2 * Z), F32)
    for a in range(3):
        for b in range(3):
            cells = jnp.concatenate(
                [coarse_in[a + x, :, b * Z : (b + 1) * Z] for x in range(2)], axis=1
            )
            total = total + dot(w_coarse[a * 3 + b], cells)
    for x in range(2):
        pre = tap_sum(total, x, CC, Z // 2, False)
        sig = sigmoid(pre)
        coarse_out[x] = (pre * sig).astype(BF)
        grad_three[x] = (cot[x].astype(F32) * (sig * (1.0 + pre * (1.0 - sig)))).astype(BF)


def grouped(taps, c):
    first = lax.broadcasted_iota(jnp.int32, (C, C // 2), 0) < C // 2
    parts = []
    for ab in range(9):
        tap = taps[ab * 3 + c].astype(F32)
        parts += [jnp.where(first, tap, 0.0), jnp.where(first, 0.0, tap)]
    return jnp.concatenate(parts, axis=1)


def back_kernel(one, two, down, coarse, one_out, two_out, down_out, coarse_out,
                w_one_t, w_two_t, w_down_t, w_coarse_t, sems):
    copies = [
        pltpu.make_async_copy(src, dst, sems.at[k])
        for k, (src, dst) in enumerate((
            (w_one_t, one_out), (w_two_t, two_out), (w_down_t, down_out), (w_coarse_t, coarse_out)
        ))
    ]
    for taps, out in ((one, w_one_t), (two, w_two_t)):
        for c in range(3):
            turned = grouped(taps, c).T
            out[c * C : (c + 1) * C, :] = jnp.concatenate(
                [turned[ab * C : (ab + 1) * C, :] for ab in range(9)], axis=1
            ).astype(BF)
    for ab in range(4):
        w_down_t[ab * C : (ab + 1) * C, :] = jnp.concatenate(
            [down[ab * 2 + c].astype(F32).T for c in range(2)], axis=1
        ).astype(BF)

    def turn(ab, carry):
        for c in range(3):
            w_coarse_t[ab, c * CD : (c + 1) * CD, :] = (
                coarse[ab, c * CC : (c + 1) * CC, :].astype(F32).T.astype(BF)
            )
        return carry

    for copy in copies[:3]:
        copy.start()
    lax.fori_loop(0, 9, turn, 0)
    copies[3].start()
    for copy in copies:
        copy.wait()


def final_kernel(core, got, other, out, out_one, out_two, out_down, wide, small, lined):
    for c in range(2):
        for mine, rows in ((True, got), (False, other)):

            @pl.when((core[0] == c) == mine)
            def _():
                for j in range(64):
                    at = c * 2048 + j * 32
                    wide[at : at + 32, :] = rows[j, :32, :].astype(F32)
                    at = c * 512 + j * 8
                    small[at : at + 8, :] = rows[j, 32:, :].astype(F32)

    for ab in range(9):
        for r in range(144):
            q, s = r // 3, r % 3
            out[ab // 3, ab % 3, :, r * Z : (r + 1) * Z] = wide[
                pl.ds(ab * 432 + s * 48 + q, 3, stride=144), :
            ]

    for base, result in ((0, out_one), (288, out_two)):
        picked = [
            jnp.concatenate(
                [small[pl.ds(base + s * 144 + k, 9, stride=16), :] for s in range(2)], axis=1
            )
            for k in range(16)
        ]
        for ab in range(9):
            line = jnp.concatenate([p[:, ab * 24 : (ab + 1) * 24] for p in picked], axis=1)
            for s in range(3):
                lined[s, :9, :] = line[:, s * Z : (s + 1) * Z]
                for k in range(3):
                    at = k * 384 + s * Z
                    result[ab // 3, ab % 3, :, at : at + Z] = lined[
                        s, pl.ds(k, 3, stride=3), :
                    ]
    picked = [
        jnp.concatenate(
            [small[pl.ds(576 + s * CD + k, 12, stride=8), :] for s in range(3)], axis=1
        )
        for k in range(8)
    ]
    for abc in range(8):
        line = jnp.concatenate([p[:, abc * C : (abc + 1) * C] for p in picked], axis=1)
        for k in range(12):
            out_down[abc // 4, abc // 2 % 2, abc % 2 : abc % 2 + 1, k * 384 : (k + 1) * 384] = line[
                k : k + 1, :
            ]


def coarse_grad_kernel(grad_three, coarse_in, out, shifted, left):
    for x in range(2):
        grad = grad_three[x].astype(F32)
        lanes = slice(x * Z, (x + 1) * Z)
        shifted[x, 0] = from_after(grad, Z // 2)
        shifted[x, 1] = grad
        shifted[x, 2] = from_before(grad, Z // 2)
        for c in range(3):
            for r in range(4):
                left[(c * 4 + r) * 48 : (c * 4 + r + 1) * 48, lanes] = shifted[
                    x, c, pl.ds(r, 48, stride=4), :
                ].astype(BF)
    for a in range(3):
        for b in range(3):
            cells = jnp.concatenate(
                [coarse_in[a + x, :, b * Z : (b + 1) * Z] for x in range(2)], axis=1
            )
            part = dot_t(left[...], cells)
            for c in range(3):
                wide = jnp.concatenate(
                    [part[(c * 4 + r) * 48 : (c * 4 + r + 1) * 48, :] for r in range(4)], axis=1
                ).astype(BF)
                tap = (a * 3 + b) * 3 + c
                for s in range(3):
                    at = (tap * 3 + s) * 48
                    out[at : at + 48, :] = wide[:, s * Z : (s + 1) * Z]
    out[81 * 48 :, :] = jnp.zeros((4096 - 81 * 48, Z), BF)


def backward_kernel(
    g_l, g_m, g_r, coarse_hbm, down_hbm, two_hbm, kept_six, kept_eight,
    mid_out, small,
    w_coarse_t, down_own, w_down_t, slope_two, act_one, w_two_t, slope_one, feat_six,
    halves, spread, mid_two, mid_one, stack, left, sems,
):
    loads = [
        pltpu.make_async_copy(src, dst, sems.at[k])
        for k, (src, dst) in enumerate((
            (coarse_hbm, w_coarse_t), (kept_eight.at[pl.ds(8, 2)], down_own),
            (down_hbm, w_down_t), (kept_eight.at[pl.ds(0, 8)], slope_two),
            (kept_six.at[pl.ds(0, 6)], act_one), (two_hbm, w_two_t),
            (kept_six.at[pl.ds(6, 6)], slope_one), (kept_six.at[pl.ds(12, 6)], feat_six),
        ))
    ]
    for load in loads:
        load.start()
    store = pltpu.make_async_copy(mid_one, mid_out, sems.at[8])
    low = low_lanes((CC, Z))

    def prepare(x, carry):
        p0, p1, p2 = g_l[x], g_m[x], g_r[x]
        s0, s1, s2 = swap_halves(p0), swap_halves(p1), swap_halves(p2)
        halves[0, x, :, :Z] = p1
        halves[0, x, :, Z:] = p2
        halves[1, x, :, :Z] = jnp.where(low, s0, s1).astype(BF)
        halves[1, x, :, Z:] = jnp.where(low, s1, s2).astype(BF)
        halves[2, x, :, :Z] = p0
        halves[2, x, :, Z:] = p1
        return carry

    lax.fori_loop(0, 6, prepare, 0)

    row = lax.broadcasted_iota(jnp.int32, (Z, 4 * Z), 0)
    col = lax.broadcasted_iota(jnp.int32, (Z, 4 * Z), 1)
    same = row // (Z // 2) == col // (2 * Z)
    place = jnp.where(same & (col % Z == 2 * (row % (Z // 2)) + (col // Z) % 2), 1.0, 0.0).astype(BF)
    low_down = low_lanes((CD, Z))

    for load in loads[:4]:
        load.wait()
    grad_down = jnp.zeros((CD, 8 * C), F32)
    for x in range(4):
        total = jnp.zeros((3 * CD, 2 * Z), F32)
        for a in range(3):
            for b in range(3):
                total = total + dot(w_coarse_t[a * 3 + b], halves[b, x + 2 - a])
        back = [tap_sum(total, k, CD, Z // 2, True).astype(BF) for k in range(2)]
        if x == 1 or x == 2:
            own = jnp.where(low_down, swap_halves(back[0]), swap_halves(back[1])).astype(BF)
            grad_down = grad_down + dot_t(own, down_own[x - 1])
        for k in range(2):
            wide = dot(back[k], place).astype(BF)
            for y in range(2):
                for c in range(2):
                    spread[c * CD : (c + 1) * CD, (k * 2 + y) * Z : (k * 2 + y + 1) * Z] = wide[
                        :, (y * 2 + c) * Z : (y * 2 + c + 1) * Z
                    ]
        fine = dot(w_down_t[...], spread[...])
        for a in range(2):
            for b in range(2):
                for y in range(4):
                    rows = slice((2 * y + b) * C, (2 * y + b + 1) * C)
                    part = fine[(a * 2 + b) * C : (a * 2 + b + 1) * C, y * Z : (y + 1) * Z]
                    mid_two[2 * x + a, rows, :] = (
                        part * slope_two[2 * x + a, rows, :].astype(F32)
                    ).astype(BF)
    for s in range(3):
        small[576 + s * CD : 576 + (s + 1) * CD, :] = grad_down[:, s * Z : (s + 1) * Z].astype(BF)

    small[864:, :] = jnp.zeros((1024 - 864, Z), BF)

    def kernel_grad(grad_of, field_of, at):
        for x in range(4):
            for y in range(4):
                lanes = slice((x * 4 + y) * Z, (x * 4 + y + 1) * Z)
                grad = grad_of(x, y).astype(F32)
                left[:C, lanes] = from_after(grad, Z).astype(BF)
                left[C : 2 * C, lanes] = grad.astype(BF)
                left[2 * C :, lanes] = from_before(grad, Z).astype(BF)
        for x in range(6):
            for y in range(6):
                piece = field_of(x, y)
                for a in range(3):
                    for b in range(3):
                        if 0 <= x - a < 4 and 0 <= y - b < 4:
                            cell = (x - a) * 4 + (y - b)
                            stack[(a * 3 + b) * C : (a * 3 + b + 1) * C, cell * Z : (cell + 1) * Z] = piece
        part = dot_t(left[...], stack[...])
        row = lax.broadcasted_iota(jnp.int32, part.shape, 0)
        col = lax.broadcasted_iota(jnp.int32, part.shape, 1)
        part = jnp.where((row % C) // 24 == (col % C) // 24, part, 0.0).astype(BF)
        row = lax.broadcasted_iota(jnp.int32, (432, 256), 0)
        col = lax.broadcasted_iota(jnp.int32, (432, 256), 1)
        fold = jnp.where((row // C == col // 24) & (row % 24 == col % 24), 1.0, 0.0).astype(BF)
        part = dot(part, fold).astype(BF)
        for s in range(2):
            small[at + s * 144 : at + (s + 1) * 144, :] = part[:, s * Z : (s + 1) * Z]

    loads[4].wait()
    kernel_grad(
        lambda x, y: mid_two[x + 2, (y + 2) * C : (y + 3) * C, :],
        lambda x, y: act_one[x, y * C : (y + 1) * C, :],
        288,
    )

    loads[5].wait()
    loads[6].wait()

    def step_two(x, carry):
        for a in range(3):
            for y in range(8):
                piece = mid_two[x + 2 - a, y * C : (y + 1) * C, :]
                for b in range(3):
                    at = y - 2 + b
                    if 0 <= at < 6:
                        stack[(a * 3 + b) * C : (a * 3 + b + 1) * C, at * Z : (at + 1) * Z] = piece
        prod = dot(w_two_t[...], stack[:, : 6 * Z])
        for y in range(6):
            rows = slice(y * C, (y + 1) * C)
            grad = tap_sum(prod, y, C, Z, True)
            mid_one[x, rows, :] = (grad * slope_one[x, rows, :].astype(F32)).astype(BF)
        return carry

    lax.fori_loop(0, 6, step_two, 0)

    store.start()
    loads[7].wait()
    kernel_grad(
        lambda x, y: mid_one[x + 1, (y + 1) * C : (y + 2) * C, :],
        lambda x, y: feat_six[x, y * C : (y + 1) * C, :],
        0,
    )
    store.wait()


def input_kernel(mid_one, w_one_t, grad_input, stack):
    def step_one(x, carry):
        for a in range(3):
            for y in range(6):
                piece = mid_one[x + 2 - a, y * C : (y + 1) * C, :]
                for b in range(3):
                    at = y - 2 + b
                    if 0 <= at < 4:
                        stack[(a * 3 + b) * C : (a * 3 + b + 1) * C, at * Z : (at + 1) * Z] = piece
        prod = dot(w_one_t[...], stack[:, : 4 * Z])
        for y in range(4):
            grad_input[x, y * C : (y + 1) * C, :] = tap_sum(prod, y, C, Z, True).astype(BF)
        return carry

    lax.fori_loop(0, 4, step_one, 0)


def call(kernel, outs, scratch, n_smem, flops, *args, far_in=(), far_out=()):
    vmem = pl.BlockSpec(memory_space=pltpu.VMEM)
    hbm = pl.BlockSpec(memory_space=pltpu.HBM)
    smem = pl.BlockSpec(memory_space=pltpu.SMEM)
    moved = sum(a.size * a.dtype.itemsize for a in args) + sum(
        o.size * o.dtype.itemsize for o in outs
    )
    return pl.pallas_call(
        kernel,
        out_shape=outs,
        in_specs=[
            smem if k < n_smem else hbm if k in far_in else vmem for k in range(len(args))
        ],
        out_specs=[hbm if k in far_out else vmem for k in range(len(outs))],
        scratch_shapes=scratch,
        compiler_params=pltpu.CompilerParams(vmem_limit_bytes=14 * 1024 * 1024),
        cost_estimate=pl.CostEstimate(flops=flops, bytes_accessed=moved, transcendentals=0),
    )(*args)


def shape(dims, dtype=BF):
    return jax.ShapeDtypeStruct(dims, dtype)


def neighbours(array, axis):
    size = lax.axis_size(axis)
    up = [(i, i + 1) for i in range(size - 1)]
    down = [(j, i) for i, j in up]
    return lax.ppermute(array, axis, up), lax.ppermute(array, axis, down)


def other_core(array):
    return lax.ppermute(array, "core", [(0, 1), (1, 0)])


def pair_sum(parts, core):
    half = parts.shape[0] // 2
    keep = lax.dynamic_slice_in_dim(parts, core * half, half, 0)
    send = lax.dynamic_slice_in_dim(parts, (1 - core) * half, half, 0)
    both = keep.astype(F32) + other_core(send).astype(F32)
    return both.astype(BF).reshape(64, half // 64, Z)


def per_device(features, conv_one, conv_two, down_weight, coarse_weight, cotangent):
    gx, gy, core = lax.axis_index("gx"), lax.axis_index(GY), lax.axis_index("core")
    last_x, last_y = lax.axis_size("gx") - 1, lax.axis_size(GY) - 1
    flags = jnp.stack([gx > 0, gx < last_x, gy > 0, gy < last_y]).astype(F32)

    feat = jnp.transpose(features, (1, 2, 0, 3)).reshape(4, 4 * C, Z)
    before, after = neighbours(feat, "gx")
    one = conv_one.reshape(27, C, C // 2)
    two = conv_two.reshape(27, C, C // 2)
    down = down_weight.reshape(8, CD, C)
    w_coarse = coarse_weight.reshape(9, 3 * CC, CD)
    before, after, one, two, down, w_coarse = lax.optimization_barrier(
        (before, after, one, two, down, w_coarse)
    )
    feat = jnp.concatenate([before, feat, after], axis=0)
    cot = jnp.transpose(cotangent.reshape(12, 16, 2, Z), (1, 0, 2, 3)).astype(BF)
    feat, cot = lax.optimization_barrier((feat, cot))
    feat_l, feat_r = neighbours(feat, GY)
    cot = lax.all_to_all(cot, "gx", 0, 0, tiled=True)

    kept_six, kept_eight, coarse_in = call(
        fine_kernel,
        [shape((18, 6 * C, Z)), shape((10, 8 * C, Z)), shape((4, CD, 3 * Z))],
        [
            pltpu.VMEM((144, 432), BF), pltpu.VMEM((144, 432), BF), pltpu.VMEM((CD, 8 * C), BF),
            pltpu.VMEM((9 * C, 10 * Z), BF), pltpu.VMEM((10, 10 * C, Z), BF),
            pltpu.VMEM((6 * C, 2 * Z), BF), pltpu.VMEM((4, 8 * C, 3 * Z), BF),
            pltpu.VMEM((6, 6 * C, Z), BF), pltpu.VMEM((8, 8 * C, Z), BF),
            pltpu.SemaphoreType.DMA((7,)),
        ],
        1, 16_000_000_000,
        flags, feat_l, feat, feat_r, one, two, down, far_out=range(2),
    )
    coarse_in, cot = lax.optimization_barrier((coarse_in, cot))
    cot = jnp.transpose(cot.reshape(CC, 2, Z), (1, 0, 2))
    coarse_out, grad_three = call(
        coarse_kernel, [shape((2, CC, Z)), shape((2, CC, Z))], [], 0, 300_000_000,
        coarse_in, w_coarse, cot,
    )

    before, after = neighbours(grad_three, "gx")
    grad_three, one, two, down, w_coarse = lax.optimization_barrier(
        (grad_three, one, two, down, w_coarse)
    )
    backs = [shape((144, 432)), shape((144, 432)), shape((4 * C, 2 * CD)), shape((9, 3 * CD, CC))]
    w_one_t, w_two_t, w_down_t, w_coarse_t = call(
        back_kernel, backs,
        [pltpu.VMEM(w.shape, BF) for w in backs] + [pltpu.SemaphoreType.DMA((4,))], 0, 0,
        one, two, down, w_coarse, far_out=range(4),
    )
    before, after, w_one_t, w_two_t, w_down_t, w_coarse_t = lax.optimization_barrier(
        (before, after, w_one_t, w_two_t, w_down_t, w_coarse_t)
    )
    wide = jnp.concatenate([before, grad_three, after], axis=0)
    g_l, g_r = neighbours(wide, GY)
    wide, grad_own = lax.optimization_barrier((wide, grad_three))
    (coarse_part,) = call(
        coarse_grad_kernel,
        [shape((4096, Z))],
        [pltpu.VMEM((2, 3, CC, Z), F32), pltpu.VMEM((3 * CC, 2 * Z), BF)],
        0, 500_000_000,
        grad_own, coarse_in,
    )
    slots = jnp.transpose(coarse_out.reshape(2, 16, 12, Z), (1, 0, 2, 3))
    slots, coarse_part = lax.optimization_barrier((slots, coarse_part))
    out = lax.all_to_all(slots, "gx", 0, 0, tiled=True)
    g_l, g_r, coarse_part = lax.optimization_barrier((g_l, g_r, coarse_part))
    coarse_mine = pair_sum(coarse_part, core)

    mid_one, small = call(
        backward_kernel,
        [shape((6, 6 * C, Z)), shape((1024, Z))],
        [
            pltpu.VMEM((9, 3 * CD, CC), BF), pltpu.VMEM((2, 8 * C, Z), BF),
            pltpu.VMEM((4 * C, 2 * CD), BF), pltpu.VMEM((8, 8 * C, Z), BF),
            pltpu.VMEM((6, 6 * C, Z), BF), pltpu.VMEM((144, 432), BF),
            pltpu.VMEM((6, 6 * C, Z), BF), pltpu.VMEM((6, 6 * C, Z), BF),
            pltpu.VMEM((3, 6, CC, 2 * Z), BF), pltpu.VMEM((2 * CD, 4 * Z), BF),
            pltpu.VMEM((8, 8 * C, Z), BF), pltpu.VMEM((6, 6 * C, Z), BF),
            pltpu.VMEM((9 * C, 16 * Z), BF), pltpu.VMEM((144, 16 * Z), BF),
            pltpu.SemaphoreType.DMA((9,)),
        ],
        0, 12_000_000_000,
        g_l, wide, g_r, w_coarse_t, w_down_t, w_two_t, kept_six, kept_eight,
        far_in=range(3, 8), far_out=(0,),
    )
    small, coarse_mine, out = lax.optimization_barrier((small, coarse_mine, out))
    parts = jnp.concatenate([coarse_mine, pair_sum(small, core)], axis=1)
    parts = lax.all_to_all(parts, SAME_CORE, 0, 0, tiled=True)
    mine = jnp.sum(parts.astype(F32), axis=0).astype(BF)
    (grad_input,) = call(
        input_kernel, [shape((4, 4 * C, Z))], [pltpu.VMEM((9 * C, 4 * Z), BF)], 0, 1_000_000_000,
        mid_one, w_one_t,
    )
    got = lax.all_to_all(
        jnp.broadcast_to(mine[None], (64,) + mine.shape), SAME_CORE, 0, 0, tiled=True
    )
    other = other_core(got)
    out = jnp.transpose(out.reshape(32, 12, Z), (1, 0, 2))
    grad_input = jnp.transpose(grad_input.reshape(4, 4, C, Z), (2, 0, 1, 3))

    grad_coarse, grad_one, grad_two, grad_down = call(
        final_kernel,
        [
            shape((3, 3, 3, CC * CD), F32), shape((3, 3, 3, C * 24), F32),
            shape((3, 3, 3, C * 24), F32), shape((2, 2, 2, CD * C), F32),
        ],
        [pltpu.VMEM((4096, Z), F32), pltpu.VMEM((1024, Z), F32), pltpu.VMEM((3, 16, Z), F32)],
        1, 0,
        core.astype(jnp.int32).reshape(1), got, other,
    )
    return out, grad_input, grad_one, grad_two, grad_down, grad_coarse


def solution(mesh):
    whole = jax.sharding.Mesh(mesh.devices.reshape(16, 4, 2), ("gx", "x", "core"))
    fine, coarse = P(None, "gx", GY, None), P("gx", None, GY)
    return jax.shard_map(
        per_device,
        mesh=whole,
        in_specs=(fine, P(), P(), P(), P(), coarse),
        out_specs=(coarse, fine, P(), P(), P(), P()),
        check_vma=False,
    )
```

```python
import jax
import jax.numpy as jnp
from jax import lax
from jax.experimental import pallas as pl
from jax.experimental.pallas import tpu as pltpu
from jax.sharding import PartitionSpec as P

BF = jnp.bfloat16
F32 = jnp.float32
C = 48
CD = 96
CC = 192
Z = 128
GY = ("x", "core")
ALL = ("gx", "x", "core")
SAME_CORE = ("gx", "x")


def dot(a, b):
    return jnp.dot(a, b, preferred_element_type=F32)


def dot_t(a, b):
    return lax.dot_general(a, b, (((1,), (1,)), ((), ())), preferred_element_type=F32)


def sigmoid(v):
    return 0.5 * jnp.tanh(0.5 * v) + 0.5


def from_before(v, segment):
    lane = lax.broadcasted_iota(jnp.int32, v.shape, 1)
    return jnp.where(lane % segment == 0, 0.0, pltpu.roll(v, 1, 1))


def from_after(v, segment):
    lane = lax.broadcasted_iota(jnp.int32, v.shape, 1)
    return jnp.where(lane % segment == segment - 1, 0.0, pltpu.roll(v, Z - 1, 1))


def tap_sum(y, lanes, rows, segment, flipped):
    one, two, three = (y[k * rows : (k + 1) * rows, lanes * Z : (lanes + 1) * Z] for k in range(3))
    if flipped:
        return from_after(one, segment) + two + from_before(three, segment)
    return from_before(one, segment) + two + from_after(three, segment)


def swap_halves(v):
    return pltpu.roll(v.astype(F32), Z // 2, 1)


def low_lanes(shape):
    return lax.broadcasted_iota(jnp.int32, shape, 1) < Z // 2


def put(taps, x, piece, y, count):
    for b in range(3):
        if 0 <= y - b < count:
            at = x * (3 * C) + b * C
            if not isinstance(x, int):
                at = pl.multiple_of(at, 16)
            taps[pl.ds(at, C), (y - b) * Z : (y - b + 1) * Z] = piece


def put_back(taps, x, piece, y, count):
    for b in range(3):
        if 0 <= y - 2 + b < count:
            at = x * (3 * C) + b * C
            if not isinstance(x, int):
                at = pl.multiple_of(at, 16)
            taps[pl.ds(at, C), (y - 2 + b) * Z : (y - 1 + b) * Z] = piece


def put_left(left, x, y, grad):
    lanes = slice(y * Z, (y + 1) * Z)
    wide = grad.astype(F32)
    left[x, :C, lanes] = from_after(wide, Z).astype(BF)
    left[x, C : 2 * C, lanes] = grad
    left[x, 2 * C :, lanes] = from_before(wide, Z).astype(BF)


def fine_kernel(
    flags, feat_l, feat_m, feat_r, one, two, down,
    kept_six, kept_eight, coarse_in,
    w_one, w_two, w_down, taps_one, taps_two, act_v, rows_two, down_all, slope_a, slope_b, sems,
):
    feats = (feat_l, feat_m, feat_r)
    inner = pl.ds(3, 6)
    copies = [
        pltpu.make_async_copy(
            feat_l.at[inner, pl.ds(3 * C, C), :], kept_six.at[pl.ds(12, 6), pl.ds(0, C), :], sems.at[0]
        ),
        pltpu.make_async_copy(
            feat_m.at[inner], kept_six.at[pl.ds(12, 6), pl.ds(C, 4 * C), :], sems.at[1]
        ),
        pltpu.make_async_copy(
            feat_r.at[inner, pl.ds(0, C), :], kept_six.at[pl.ds(12, 6), pl.ds(5 * C, C), :], sems.at[2]
        ),
        pltpu.make_async_copy(
            act_v.at[pl.ds(2, 6)], kept_six.at[pl.ds(0, 6)], sems.at[3]
        ),
        pltpu.make_async_copy(
            slope_a.at[pl.ds(2, 6)], kept_six.at[pl.ds(6, 6)], sems.at[4]
        ),
        pltpu.make_async_copy(slope_b, kept_eight.at[pl.ds(0, 8)], sems.at[5]),
        pltpu.make_async_copy(
            down_all.at[pl.ds(1, 2), :, pl.ds(Z, Z)], kept_eight.at[pl.ds(8, 2)], sems.at[6]
        ),
    ]
    for copy in copies[:3]:
        copy.start()
    for taps, w in ((one, w_one), (two, w_two)):
        for c in range(3):
            w[c * C : (c + 1) * C, :] = grouped(taps, c).astype(BF)
    w_down[...] = jnp.concatenate([down[k].astype(F32) for k in range(8)], axis=1).astype(BF)

    def valid(x, lo, hi):
        ok_l = jnp.where(x < lo, flags[0], 1.0)
        return jnp.where(x >= hi, flags[1], ok_l)

    def valid_y(y, lo, hi):
        if y < lo:
            return flags[2]
        if y >= hi:
            return flags[3]
        return 1.0

    def spread_one(x, carry):
        for y in range(12):
            piece = feats[y // 4][x, (y % 4) * C : (y % 4 + 1) * C, :]
            put(taps_one, x, piece, y, 10)
        return carry

    lax.fori_loop(0, 12, spread_one, 0, unroll=2)

    def step_one(x, carry):
        prod = dot(w_one[...], taps_one[pl.ds(pl.multiple_of(x * 3 * C, 16), 9 * C), :])
        ok_x = valid(x, 3, 7)
        for y in range(10):
            pre = tap_sum(prod, y, C, Z, False)
            sig = sigmoid(pre)
            ok = ok_x * valid_y(y, 3, 7)
            act = (pre * sig * ok).astype(BF)
            put(taps_two, x, act, y, 8)
            if 2 <= y < 8:
                slp = (sig * (1.0 + pre * (1.0 - sig)) * ok).astype(BF)

                act_v[x, (y - 2) * C : (y - 1) * C, :] = act
                slope_a[x, (y - 2) * C : (y - 1) * C, :] = slp
        return carry

    lax.fori_loop(0, 10, step_one, 0, unroll=5)
    copies[3].start()
    copies[4].start()

    row = lax.broadcasted_iota(jnp.int32, (2 * Z, 2 * Z), 0)
    col = lax.broadcasted_iota(jnp.int32, (2 * Z, 2 * Z), 1)
    same = (row // Z) == (col % Z) // (Z // 2)
    select = jnp.where(same & (row % Z == 2 * (col % (Z // 2)) + col // Z), 1.0, 0.0).astype(BF)

    def step_two(x, carry):
        prod = dot(w_two[...], taps_two[pl.ds(pl.multiple_of(x * 3 * C, 16), 9 * C), :])
        ok_x = valid(x, 2, 6)
        for y in range(8):
            pre = tap_sum(prod, y, C, Z, False)
            sig = sigmoid(pre)
            ok = ok_x * valid_y(y, 2, 6)
            act = (pre * sig * ok).astype(BF)
            slope_b[x, y * C : (y + 1) * C, :] = (sig * (1.0 + pre * (1.0 - sig)) * ok).astype(BF)
            pair, b = y // 2, y % 2
            if pair < 3:
                rows_two[(pair * 2 + b) * C : (pair * 2 + b + 1) * C, :Z] = act
            if pair > 0:
                rows_two[((pair - 1) * 2 + b) * C : ((pair - 1) * 2 + b + 1) * C, Z:] = act
        picked = dot(rows_two[...], select).astype(BF)
        a = x % 2
        for pair in range(3):
            for b in range(2):
                for c in range(2):
                    at = pl.multiple_of(a * (4 * C) + (b * 2 + c) * C, 16)
                    down_all[x // 2, pl.ds(at, C), pair * Z : (pair + 1) * Z] = picked[
                        (pair * 2 + b) * C : (pair * 2 + b + 1) * C, c * Z : (c + 1) * Z
                    ]
        return carry

    lax.fori_loop(0, 8, step_two, 0, unroll=4)
    copies[5].start()
    copies[6].start()
    for x in range(4):
        coarse_in[x] = dot(w_down[...], down_all[x]).astype(BF)
    for copy in copies:
        copy.wait()


def coarse_kernel(coarse_in, w_coarse, cot, coarse_out, grad_three):
    total = jnp.zeros((3 * CC, 2 * Z), F32)
    for a in range(3):
        for b in range(3):
            cells = jnp.concatenate(
                [coarse_in[a + x, :, b * Z : (b + 1) * Z] for x in range(2)], axis=1
            )
            total = total + dot(w_coarse[a * 3 + b], cells)
    for x in range(2):
        pre = tap_sum(total, x, CC, Z // 2, False)
        sig = sigmoid(pre)
        coarse_out[x] = (pre * sig).astype(BF)
        grad_three[x] = (cot[x].astype(F32) * (sig * (1.0 + pre * (1.0 - sig)))).astype(BF)


def grouped(taps, c):
    first = lax.broadcasted_iota(jnp.int32, (C, C // 2), 0) < C // 2
    parts = []
    for ab in range(9):
        tap = taps[ab * 3 + c].astype(F32)
        parts += [jnp.where(first, tap, 0.0), jnp.where(first, 0.0, tap)]
    return jnp.concatenate(parts, axis=1)


def back_kernel(one, two, down, coarse, one_out, two_out, down_out, coarse_out,
                w_one_t, w_two_t, w_down_t, w_coarse_t, sems):
    copies = [
        pltpu.make_async_copy(src, dst, sems.at[k])
        for k, (src, dst) in enumerate((
            (w_one_t, one_out), (w_two_t, two_out), (w_down_t, down_out), (w_coarse_t, coarse_out)
        ))
    ]
    for taps, out in ((one, w_one_t), (two, w_two_t)):
        for c in range(3):
            turned = grouped(taps, c).T
            out[c * C : (c + 1) * C, :] = jnp.concatenate(
                [
                    turned[ab * C : (ab + 1) * C, :]
                    for ab in (6, 7, 8, 3, 4, 5, 0, 1, 2)
                ],
                axis=1,
            ).astype(BF)
    for ab in range(4):
        w_down_t[ab * C : (ab + 1) * C, :] = jnp.concatenate(
            [down[ab * 2 + c].astype(F32).T for c in range(2)], axis=1
        ).astype(BF)

    def turn(ab, carry):
        for c in range(3):
            w_coarse_t[ab, c * CD : (c + 1) * CD, :] = (
                coarse[ab, c * CC : (c + 1) * CC, :].astype(F32).T.astype(BF)
            )
        return carry

    for copy in copies[:3]:
        copy.start()
    lax.fori_loop(0, 9, turn, 0)
    copies[3].start()
    for copy in copies:
        copy.wait()


def final_kernel(core, got, other, out, out_one, out_two, out_down, wide, small, lined):
    for c in range(2):
        for mine, rows in ((True, got), (False, other)):

            @pl.when((core[0] == c) == mine)
            def _():
                for j in range(64):
                    at = c * 2048 + j * 32
                    wide[at : at + 32, :] = rows[j, :32, :].astype(F32)
                    at = c * 512 + j * 8
                    small[at : at + 8, :] = rows[j, 32:, :].astype(F32)

    for ab in range(9):
        for r in range(144):
            q, s = r // 3, r % 3
            out[ab // 3, ab % 3, :, r * Z : (r + 1) * Z] = wide[
                pl.ds(ab * 432 + s * 48 + q, 3, stride=144), :
            ]

    for base, result in ((0, out_one), (288, out_two)):
        picked = [
            jnp.concatenate(
                [small[pl.ds(base + s * 144 + k, 9, stride=16), :] for s in range(2)], axis=1
            )
            for k in range(16)
        ]
        for ab in range(9):
            line = jnp.concatenate([p[:, ab * 24 : (ab + 1) * 24] for p in picked], axis=1)
            for s in range(3):
                lined[s, :9, :] = line[:, s * Z : (s + 1) * Z]
                for k in range(3):
                    at = k * 384 + s * Z
                    result[ab // 3, ab % 3, :, at : at + Z] = lined[
                        s, pl.ds(k, 3, stride=3), :
                    ]
    picked = [
        jnp.concatenate(
            [small[pl.ds(576 + s * CD + k, 12, stride=8), :] for s in range(3)], axis=1
        )
        for k in range(8)
    ]
    for abc in range(8):
        line = jnp.concatenate([p[:, abc * C : (abc + 1) * C] for p in picked], axis=1)
        for k in range(12):
            out_down[abc // 4, abc // 2 % 2, abc % 2 : abc % 2 + 1, k * 384 : (k + 1) * 384] = line[
                k : k + 1, :
            ]


def coarse_grad_kernel(grad_three, coarse_in, out, shifted, left):
    for x in range(2):
        grad = grad_three[x].astype(F32)
        lanes = slice(x * Z, (x + 1) * Z)
        shifted[x, 0] = from_after(grad, Z // 2)
        shifted[x, 1] = grad
        shifted[x, 2] = from_before(grad, Z // 2)
        for c in range(3):
            for r in range(4):
                left[(c * 4 + r) * 48 : (c * 4 + r + 1) * 48, lanes] = shifted[
                    x, c, pl.ds(r, 48, stride=4), :
                ].astype(BF)
    for a in range(3):
        for b in range(3):
            cells = jnp.concatenate(
                [coarse_in[a + x, :, b * Z : (b + 1) * Z] for x in range(2)], axis=1
            )
            part = dot_t(left[...], cells)
            for c in range(3):
                wide = jnp.concatenate(
                    [part[(c * 4 + r) * 48 : (c * 4 + r + 1) * 48, :] for r in range(4)], axis=1
                ).astype(BF)
                tap = (a * 3 + b) * 3 + c
                for s in range(3):
                    at = (tap * 3 + s) * 48
                    out[at : at + 48, :] = wide[:, s * Z : (s + 1) * Z]
    out[81 * 48 :, :] = jnp.zeros((4096 - 81 * 48, Z), BF)


def backward_kernel(
    g_l, g_m, g_r, coarse_hbm, down_hbm, two_hbm, kept_six, kept_eight,
    mid_out, small,
    w_coarse_t, down_own, w_down_t, slope_two, act_one, w_two_t, slope_one, feat_six,
    halves, spread, mid_one, taps, taps_mid, left, sems,
):
    loads = [
        pltpu.make_async_copy(src, dst, sems.at[k])
        for k, (src, dst) in enumerate((
            (coarse_hbm, w_coarse_t), (kept_eight.at[pl.ds(8, 2)], down_own),
            (down_hbm, w_down_t), (kept_eight.at[pl.ds(0, 8)], slope_two),
            (kept_six.at[pl.ds(0, 6)], act_one), (two_hbm, w_two_t),
            (kept_six.at[pl.ds(6, 6)], slope_one), (kept_six.at[pl.ds(12, 6)], feat_six),
        ))
    ]
    for load in loads:
        load.start()
    store = pltpu.make_async_copy(mid_one, mid_out, sems.at[8])
    low = low_lanes((CC, Z))

    def prepare(x, carry):
        p0, p1, p2 = g_l[x], g_m[x], g_r[x]
        s0, s1, s2 = swap_halves(p0), swap_halves(p1), swap_halves(p2)
        halves[0, x, :, :Z] = p1
        halves[0, x, :, Z:] = p2
        halves[1, x, :, :Z] = jnp.where(low, s0, s1).astype(BF)
        halves[1, x, :, Z:] = jnp.where(low, s1, s2).astype(BF)
        halves[2, x, :, :Z] = p0
        halves[2, x, :, Z:] = p1
        return carry

    lax.fori_loop(0, 6, prepare, 0)

    row = lax.broadcasted_iota(jnp.int32, (Z, 4 * Z), 0)
    col = lax.broadcasted_iota(jnp.int32, (Z, 4 * Z), 1)
    same = row // (Z // 2) == col // (2 * Z)
    place = jnp.where(same & (col % Z == 2 * (row % (Z // 2)) + (col // Z) % 2), 1.0, 0.0).astype(BF)
    low_down = low_lanes((CD, Z))

    for load in loads[:4]:
        load.wait()
    grad_down = jnp.zeros((CD, 8 * C), F32)
    for x in range(4):
        total = jnp.zeros((3 * CD, 2 * Z), F32)
        for a in range(3):
            for b in range(3):
                total = total + dot(w_coarse_t[a * 3 + b], halves[b, x + 2 - a])
        back = [tap_sum(total, k, CD, Z // 2, True).astype(BF) for k in range(2)]
        if x == 1 or x == 2:
            own = jnp.where(low_down, swap_halves(back[0]), swap_halves(back[1])).astype(BF)
            grad_down = grad_down + dot_t(own, down_own[x - 1])
        for k in range(2):
            wide = dot(back[k], place).astype(BF)
            for y in range(2):
                for c in range(2):
                    spread[c * CD : (c + 1) * CD, (k * 2 + y) * Z : (k * 2 + y + 1) * Z] = wide[
                        :, (y * 2 + c) * Z : (y * 2 + c + 1) * Z
                    ]
        fine = dot(w_down_t[...], spread[...])
        for a in range(2):
            for b in range(2):
                for y in range(4):
                    rows = slice((2 * y + b) * C, (2 * y + b + 1) * C)
                    part = fine[(a * 2 + b) * C : (a * 2 + b + 1) * C, y * Z : (y + 1) * Z]
                    mid = (part * slope_two[2 * x + a, rows, :].astype(F32)).astype(BF)
                    put_back(taps_mid, 2 * x + a, mid, 2 * y + b, 6)
                    if 0 < x < 3 and 0 < y < 3:
                        put_left(left, 2 * x + a - 2, 2 * y + b - 2, mid)
    for s in range(3):
        small[576 + s * CD : 576 + (s + 1) * CD, :] = grad_down[:, s * Z : (s + 1) * Z].astype(BF)

    small[864:, :] = jnp.zeros((1024 - 864, Z), BF)

    def kernel_grad(field, at):
        for x in range(6):
            for y in range(6):
                put(taps, x, field[x, y * C : (y + 1) * C, :], y, 4)
        part = jnp.zeros((3 * C, 9 * C), F32)
        for x in range(4):
            part = part + dot_t(left[x], taps[x * 3 * C : (x + 3) * 3 * C, :])
        row = lax.broadcasted_iota(jnp.int32, part.shape, 0)
        col = lax.broadcasted_iota(jnp.int32, part.shape, 1)
        part = jnp.where((row % C) // 24 == (col % C) // 24, part, 0.0).astype(BF)
        row = lax.broadcasted_iota(jnp.int32, (432, 256), 0)
        col = lax.broadcasted_iota(jnp.int32, (432, 256), 1)
        fold = jnp.where((row // C == col // 24) & (row % 24 == col % 24), 1.0, 0.0).astype(BF)
        part = dot(part, fold).astype(BF)
        for s in range(2):
            small[at + s * 144 : at + (s + 1) * 144, :] = part[:, s * Z : (s + 1) * Z]

    loads[4].wait()
    kernel_grad(act_one, 288)

    loads[5].wait()
    loads[6].wait()

    def step_two(x, carry):
        prod = dot(w_two_t[...], taps_mid[pl.ds(pl.multiple_of(x * 3 * C, 16), 9 * C), :])
        for y in range(6):
            rows = slice(y * C, (y + 1) * C)
            grad = tap_sum(prod, y, C, Z, True)
            mid = (grad * slope_one[x, rows, :].astype(F32)).astype(BF)
            mid_one[x, rows, :] = mid
        return carry

    lax.fori_loop(0, 6, step_two, 0, unroll=3)

    store.start()
    for x in range(4):
        for y in range(4):
            put_left(left, x, y, mid_one[x + 1, (y + 1) * C : (y + 2) * C, :])
    loads[7].wait()
    kernel_grad(feat_six, 0)
    store.wait()


def input_kernel(mid_one, w_one_t, grad_input, taps):
    for x in range(6):
        for y in range(6):
            put_back(taps, x, mid_one[x, y * C : (y + 1) * C, :], y, 4)
    for x in range(4):
        prod = dot(w_one_t[...], taps[x * 3 * C : (x + 3) * 3 * C, :])
        for y in range(4):
            grad_input[x, y * C : (y + 1) * C, :] = tap_sum(prod, y, C, Z, True).astype(BF)


def call(kernel, outs, scratch, n_smem, flops, *args, far_in=(), far_out=(), limit=20):
    vmem = pl.BlockSpec(memory_space=pltpu.VMEM)
    hbm = pl.BlockSpec(memory_space=pltpu.HBM)
    smem = pl.BlockSpec(memory_space=pltpu.SMEM)
    moved = sum(a.size * a.dtype.itemsize for a in args) + sum(
        o.size * o.dtype.itemsize for o in outs
    )
    return pl.pallas_call(
        kernel,
        out_shape=outs,
        in_specs=[
            smem if k < n_smem else hbm if k in far_in else vmem for k in range(len(args))
        ],
        out_specs=[hbm if k in far_out else vmem for k in range(len(outs))],
        scratch_shapes=scratch,
        compiler_params=pltpu.CompilerParams(vmem_limit_bytes=limit * 1024 * 1024),
        cost_estimate=pl.CostEstimate(flops=flops, bytes_accessed=moved, transcendentals=0),
    )(*args)


def shape(dims, dtype=BF):
    return jax.ShapeDtypeStruct(dims, dtype)


def neighbours(array, axis):
    size = lax.axis_size(axis)
    up = [(i, i + 1) for i in range(size - 1)]
    down = [(j, i) for i, j in up]
    return lax.ppermute(array, axis, up), lax.ppermute(array, axis, down)


def other_core(array):
    return lax.ppermute(array, "core", [(0, 1), (1, 0)])


def pair_sum(parts, core):
    half = parts.shape[0] // 2
    keep = lax.dynamic_slice_in_dim(parts, core * half, half, 0)
    send = lax.dynamic_slice_in_dim(parts, (1 - core) * half, half, 0)
    both = keep.astype(F32) + other_core(send).astype(F32)
    return both.astype(BF).reshape(64, half // 64, Z)


def per_device(features, conv_one, conv_two, down_weight, coarse_weight, cotangent):
    gx, gy, core = lax.axis_index("gx"), lax.axis_index(GY), lax.axis_index("core")
    last_x, last_y = lax.axis_size("gx") - 1, lax.axis_size(GY) - 1
    flags = jnp.stack([gx > 0, gx < last_x, gy > 0, gy < last_y]).astype(F32)

    feat = jnp.transpose(features, (1, 2, 0, 3)).reshape(4, 4 * C, Z)
    before, after = neighbours(feat, "gx")
    one = conv_one.reshape(27, C, C // 2)
    two = conv_two.reshape(27, C, C // 2)
    down = down_weight.reshape(8, CD, C)
    w_coarse = coarse_weight.reshape(9, 3 * CC, CD)
    before, after, one, two, down, w_coarse = lax.optimization_barrier(
        (before, after, one, two, down, w_coarse)
    )
    feat = jnp.concatenate([before, feat, after], axis=0)
    cot = jnp.transpose(cotangent.reshape(12, 16, 2, Z), (1, 0, 2, 3)).astype(BF)
    feat, cot = lax.optimization_barrier((feat, cot))
    feat_l, feat_r = neighbours(feat, GY)
    cot = lax.all_to_all(cot, "gx", 0, 0, tiled=True)

    kept_six, kept_eight, coarse_in = call(
        fine_kernel,
        [shape((18, 6 * C, Z)), shape((10, 8 * C, Z)), shape((4, CD, 3 * Z))],
        [
            pltpu.VMEM((144, 432), BF), pltpu.VMEM((144, 432), BF), pltpu.VMEM((CD, 8 * C), BF),
            pltpu.VMEM((36 * C, 10 * Z), BF), pltpu.VMEM((30 * C, 8 * Z), BF),
            pltpu.VMEM((10, 6 * C, Z), BF), pltpu.VMEM((6 * C, 2 * Z), BF), pltpu.VMEM((4, 8 * C, 3 * Z), BF),
            pltpu.VMEM((10, 6 * C, Z), BF), pltpu.VMEM((8, 8 * C, Z), BF),
            pltpu.SemaphoreType.DMA((7,)),
        ],
        1, 16_000_000_000,
        flags, feat_l, feat, feat_r, one, two, down, far_out=range(2), limit=20,
    )
    coarse_in, cot = lax.optimization_barrier((coarse_in, cot))
    cot = jnp.transpose(cot.reshape(CC, 2, Z), (1, 0, 2))
    coarse_out, grad_three = call(
        coarse_kernel, [shape((2, CC, Z)), shape((2, CC, Z))], [], 0, 300_000_000,
        coarse_in, w_coarse, cot,
    )

    before, after = neighbours(grad_three, "gx")
    grad_three, one, two, down, w_coarse = lax.optimization_barrier(
        (grad_three, one, two, down, w_coarse)
    )
    backs = [shape((144, 432)), shape((144, 432)), shape((4 * C, 2 * CD)), shape((9, 3 * CD, CC))]
    w_one_t, w_two_t, w_down_t, w_coarse_t = call(
        back_kernel, backs,
        [pltpu.VMEM(w.shape, BF) for w in backs] + [pltpu.SemaphoreType.DMA((4,))], 0, 0,
        one, two, down, w_coarse, far_out=range(4), limit=20,
    )
    before, after, w_one_t, w_two_t, w_down_t, w_coarse_t = lax.optimization_barrier(
        (before, after, w_one_t, w_two_t, w_down_t, w_coarse_t)
    )
    wide = jnp.concatenate([before, grad_three, after], axis=0)
    g_l, g_r = neighbours(wide, GY)
    wide, grad_own = lax.optimization_barrier((wide, grad_three))
    (coarse_part,) = call(
        coarse_grad_kernel,
        [shape((4096, Z))],
        [pltpu.VMEM((2, 3, CC, Z), F32), pltpu.VMEM((3 * CC, 2 * Z), BF)],
        0, 500_000_000,
        grad_own, coarse_in,
    )
    slots = jnp.transpose(coarse_out.reshape(2, 16, 12, Z), (1, 0, 2, 3))
    slots, coarse_part = lax.optimization_barrier((slots, coarse_part))
    out = lax.all_to_all(slots, "gx", 0, 0, tiled=True)
    g_l, g_r, coarse_part = lax.optimization_barrier((g_l, g_r, coarse_part))
    coarse_mine = pair_sum(coarse_part, core)

    mid_one, small = call(
        backward_kernel,
        [shape((6, 6 * C, Z)), shape((1024, Z))],
        [
            pltpu.VMEM((9, 3 * CD, CC), BF), pltpu.VMEM((2, 8 * C, Z), BF),
            pltpu.VMEM((4 * C, 2 * CD), BF), pltpu.VMEM((8, 8 * C, Z), BF),
            pltpu.VMEM((6, 6 * C, Z), BF), pltpu.VMEM((144, 432), BF),
            pltpu.VMEM((6, 6 * C, Z), BF), pltpu.VMEM((6, 6 * C, Z), BF),
            pltpu.VMEM((3, 6, CC, 2 * Z), BF), pltpu.VMEM((2 * CD, 4 * Z), BF),
            pltpu.VMEM((6, 6 * C, Z), BF), pltpu.VMEM((18 * C, 4 * Z), BF),
            pltpu.VMEM((24 * C, 6 * Z), BF), pltpu.VMEM((4, 3 * C, 4 * Z), BF),
            pltpu.SemaphoreType.DMA((9,)),
        ],
        0, 12_000_000_000,
        g_l, wide, g_r, w_coarse_t, w_down_t, w_two_t, kept_six, kept_eight,
        far_in=range(3, 8), far_out=(0,), limit=58,
    )
    small, coarse_mine, out = lax.optimization_barrier((small, coarse_mine, out))
    parts = jnp.concatenate([coarse_mine, pair_sum(small, core)], axis=1)
    parts = lax.all_to_all(parts, SAME_CORE, 0, 0, tiled=True)
    mine = jnp.sum(parts.astype(F32), axis=0).astype(BF)
    (grad_input,) = call(
        input_kernel, [shape((4, 4 * C, Z))], [pltpu.VMEM((18 * C, 4 * Z), BF)], 0, 1_000_000_000,
        mid_one, w_one_t,
    )
    got = lax.all_to_all(
        jnp.broadcast_to(mine[None], (64,) + mine.shape), SAME_CORE, 0, 0, tiled=True
    )
    other = other_core(got)
    out = jnp.transpose(out.reshape(32, 12, Z), (1, 0, 2))
    grad_input = jnp.transpose(grad_input.reshape(4, 4, C, Z), (2, 0, 1, 3))

    grad_coarse, grad_one, grad_two, grad_down = call(
        final_kernel,
        [
            shape((3, 3, 3, CC * CD), F32), shape((3, 3, 3, C * 24), F32),
            shape((3, 3, 3, C * 24), F32), shape((2, 2, 2, CD * C), F32),
        ],
        [pltpu.VMEM((4096, Z), F32), pltpu.VMEM((1024, Z), F32), pltpu.VMEM((3, 16, Z), F32)],
        1, 0,
        core.astype(jnp.int32).reshape(1), got, other,
    )
    return out, grad_input, grad_one, grad_two, grad_down, grad_coarse


def solution(mesh):
    whole = jax.sharding.Mesh(mesh.devices.reshape(16, 4, 2), ("gx", "x", "core"))
    fine, coarse = P(None, "gx", GY, None), P("gx", None, GY)
    return jax.shard_map(
        per_device,
        mesh=whole,
        in_specs=(fine, P(), P(), P(), P(), coarse),
        out_specs=(coarse, fine, P(), P(), P(), P()),
        check_vma=False,
    )
```

```python
import jax
import jax.numpy as jnp
from jax import lax
from jax.experimental import pallas as pl
from jax.experimental.pallas import tpu as pltpu
from jax.sharding import PartitionSpec as P

BF = jnp.bfloat16
F32 = jnp.float32
C = 48
CD = 96
CC = 192
Z = 128
GY = ("x", "core")
ALL = ("gx", "x", "core")
SAME_CORE = ("gx", "x")


def dot(a, b):
    return jnp.dot(a, b, preferred_element_type=F32)


def dot_t(a, b):
    return lax.dot_general(a, b, (((1,), (1,)), ((), ())), preferred_element_type=F32)


def sigmoid(v):
    return 0.5 * jnp.tanh(0.5 * v) + 0.5


def from_before(v, segment):
    lane = lax.broadcasted_iota(jnp.int32, v.shape, 1)
    return jnp.where(lane % segment == 0, 0.0, pltpu.roll(v, 1, 1))


def from_after(v, segment):
    lane = lax.broadcasted_iota(jnp.int32, v.shape, 1)
    return jnp.where(lane % segment == segment - 1, 0.0, pltpu.roll(v, Z - 1, 1))


def tap_sum(y, lanes, rows, segment, flipped):
    one, two, three = (y[k * rows : (k + 1) * rows, lanes * Z : (lanes + 1) * Z] for k in range(3))
    if flipped:
        return from_after(one, segment) + two + from_before(three, segment)
    return from_before(one, segment) + two + from_after(three, segment)


def swap_halves(v):
    return pltpu.roll(v.astype(F32), Z // 2, 1)


def low_lanes(shape):
    return lax.broadcasted_iota(jnp.int32, shape, 1) < Z // 2


def put(taps, x, piece, y, count):
    for b in range(3):
        if 0 <= y - b < count:
            at = x * (3 * C) + b * C
            if not isinstance(x, int):
                at = pl.multiple_of(at, 16)
            taps[pl.ds(at, C), (y - b) * Z : (y - b + 1) * Z] = piece


def put_back(taps, x, piece, y, count):
    for b in range(3):
        if 0 <= y - 2 + b < count:
            at = x * (3 * C) + b * C
            if not isinstance(x, int):
                at = pl.multiple_of(at, 16)
            taps[pl.ds(at, C), (y - 2 + b) * Z : (y - 1 + b) * Z] = piece


def put_left(left, x, y, grad):
    lanes = slice(y * Z, (y + 1) * Z)
    wide = grad.astype(F32)
    left[x, :C, lanes] = from_after(wide, Z).astype(BF)
    left[x, C : 2 * C, lanes] = grad
    left[x, 2 * C :, lanes] = from_before(wide, Z).astype(BF)


def fine_kernel(
    flags, feat_l, feat_m, feat_r, one, two, down,
    kept_six, kept_eight, coarse_in,
    w_one, w_two, w_down, taps_one, taps_two, act_v, rows_two, down_all, slope_a, slope_b, sems,
):
    feats = (feat_l, feat_m, feat_r)
    inner = pl.ds(3, 6)
    copies = [
        pltpu.make_async_copy(
            feat_l.at[inner, pl.ds(3 * C, C), :], kept_six.at[pl.ds(12, 6), pl.ds(0, C), :], sems.at[0]
        ),
        pltpu.make_async_copy(
            feat_m.at[inner], kept_six.at[pl.ds(12, 6), pl.ds(C, 4 * C), :], sems.at[1]
        ),
        pltpu.make_async_copy(
            feat_r.at[inner, pl.ds(0, C), :], kept_six.at[pl.ds(12, 6), pl.ds(5 * C, C), :], sems.at[2]
        ),
        pltpu.make_async_copy(
            act_v.at[pl.ds(2, 6)], kept_six.at[pl.ds(0, 6)], sems.at[3]
        ),
        pltpu.make_async_copy(
            slope_a.at[pl.ds(2, 6)], kept_six.at[pl.ds(6, 6)], sems.at[4]
        ),
        pltpu.make_async_copy(slope_b, kept_eight.at[pl.ds(0, 8)], sems.at[5]),
        pltpu.make_async_copy(
            down_all.at[pl.ds(1, 2), :, pl.ds(Z, Z)], kept_eight.at[pl.ds(8, 2)], sems.at[6]
        ),
    ]
    for copy in copies[:3]:
        copy.start()
    for taps, w in ((one, w_one), (two, w_two)):
        for c in range(3):
            w[c * C : (c + 1) * C, :] = grouped(taps, c).astype(BF)
    w_down[...] = jnp.concatenate([down[k].astype(F32) for k in range(8)], axis=1).astype(BF)

    def valid(x, lo, hi):
        ok_l = jnp.where(x < lo, flags[0], 1.0)
        return jnp.where(x >= hi, flags[1], ok_l)

    def valid_y(y, lo, hi):
        if y < lo:
            return flags[2]
        if y >= hi:
            return flags[3]
        return 1.0

    def spread_one(x, carry):
        for y in range(12):
            piece = feats[y // 4][x, (y % 4) * C : (y % 4 + 1) * C, :]
            put(taps_one, x, piece, y, 10)
        return carry

    lax.fori_loop(0, 12, spread_one, 0, unroll=2)

    def step_one(x, carry):
        prod = dot(w_one[...], taps_one[pl.ds(pl.multiple_of(x * 3 * C, 16), 9 * C), :])
        ok_x = valid(x, 3, 7)
        for y in range(10):
            pre = tap_sum(prod, y, C, Z, False)
            sig = sigmoid(pre)
            ok = ok_x * valid_y(y, 3, 7)
            act = (pre * sig * ok).astype(BF)
            put(taps_two, x, act, y, 8)
            if 2 <= y < 8:
                slp = (sig * (1.0 + pre * (1.0 - sig)) * ok).astype(BF)

                act_v[x, (y - 2) * C : (y - 1) * C, :] = act
                slope_a[x, (y - 2) * C : (y - 1) * C, :] = slp
        return carry

    lax.fori_loop(0, 10, step_one, 0, unroll=5)
    copies[3].start()
    copies[4].start()

    row = lax.broadcasted_iota(jnp.int32, (2 * Z, 2 * Z), 0)
    col = lax.broadcasted_iota(jnp.int32, (2 * Z, 2 * Z), 1)
    same = (row // Z) == (col % Z) // (Z // 2)
    select = jnp.where(same & (row % Z == 2 * (col % (Z // 2)) + col // Z), 1.0, 0.0).astype(BF)

    def step_two(x, carry):
        prod = dot(w_two[...], taps_two[pl.ds(pl.multiple_of(x * 3 * C, 16), 9 * C), :])
        ok_x = valid(x, 2, 6)
        for y in range(8):
            pre = tap_sum(prod, y, C, Z, False)
            sig = sigmoid(pre)
            ok = ok_x * valid_y(y, 2, 6)
            act = (pre * sig * ok).astype(BF)
            slope_b[x, y * C : (y + 1) * C, :] = (sig * (1.0 + pre * (1.0 - sig)) * ok).astype(BF)
            pair, b = y // 2, y % 2
            if pair < 3:
                rows_two[(pair * 2 + b) * C : (pair * 2 + b + 1) * C, :Z] = act
            if pair > 0:
                rows_two[((pair - 1) * 2 + b) * C : ((pair - 1) * 2 + b + 1) * C, Z:] = act
        picked = dot(rows_two[...], select).astype(BF)
        a = x % 2
        for pair in range(3):
            for b in range(2):
                for c in range(2):
                    at = pl.multiple_of(a * (4 * C) + (b * 2 + c) * C, 16)
                    down_all[x // 2, pl.ds(at, C), pair * Z : (pair + 1) * Z] = picked[
                        (pair * 2 + b) * C : (pair * 2 + b + 1) * C, c * Z : (c + 1) * Z
                    ]
        return carry

    lax.fori_loop(0, 8, step_two, 0, unroll=4)
    copies[5].start()
    copies[6].start()
    for x in range(4):
        coarse_in[x] = dot(w_down[...], down_all[x]).astype(BF)
    for copy in copies:
        copy.wait()


def coarse_kernel(coarse_in, w_coarse, cot, coarse_out, grad_three):
    total = jnp.zeros((3 * CC, 2 * Z), F32)
    for a in range(3):
        for b in range(3):
            cells = jnp.concatenate(
                [coarse_in[a + x, :, b * Z : (b + 1) * Z] for x in range(2)], axis=1
            )
            total = total + dot(w_coarse[a * 3 + b], cells)
    for x in range(2):
        pre = tap_sum(total, x, CC, Z // 2, False)
        sig = sigmoid(pre)
        coarse_out[x] = (pre * sig).astype(BF)
        grad_three[x] = (cot[x].astype(F32) * (sig * (1.0 + pre * (1.0 - sig)))).astype(BF)


def grouped(taps, c):
    first = lax.broadcasted_iota(jnp.int32, (C, C // 2), 0) < C // 2
    parts = []
    for ab in range(9):
        tap = taps[ab * 3 + c].astype(F32)
        parts += [jnp.where(first, tap, 0.0), jnp.where(first, 0.0, tap)]
    return jnp.concatenate(parts, axis=1)


def back_kernel(one, two, down, coarse, one_out, two_out, down_out, coarse_out,
                w_one_t, w_two_t, w_down_t, w_coarse_t, sems):
    copies = [
        pltpu.make_async_copy(src, dst, sems.at[k])
        for k, (src, dst) in enumerate((
            (w_one_t, one_out), (w_two_t, two_out), (w_down_t, down_out), (w_coarse_t, coarse_out.at[pl.ds(0, 9)])
        ))
    ]
    for taps, out in ((one, w_one_t), (two, w_two_t)):
        for c in range(3):
            turned = grouped(taps, c).T
            out[c * C : (c + 1) * C, :] = jnp.concatenate(
                [
                    turned[ab * C : (ab + 1) * C, :]
                    for ab in (6, 7, 8, 3, 4, 5, 0, 1, 2)
                ],
                axis=1,
            ).astype(BF)
    for ab in range(4):
        w_down_t[ab * C : (ab + 1) * C, :] = jnp.concatenate(
            [down[ab * 2 + c].astype(F32).T for c in range(2)], axis=1
        ).astype(BF)

    def turn(ab, carry):
        for c in range(3):
            w_coarse_t[ab, c * CD : (c + 1) * CD, :] = (
                coarse[ab, c * CC : (c + 1) * CC, :].astype(F32).T.astype(BF)
            )
        return carry

    for copy in copies[:3]:
        copy.start()
    lax.fori_loop(0, 9, turn, 0)
    copies[3].start()
    for copy in copies:
        copy.wait()


def final_kernel(core, got, other, out, out_one, out_two, out_down, wide, small, lined):
    for c in range(2):
        for mine, rows in ((True, got), (False, other)):

            @pl.when((core[0] == c) == mine)
            def _():
                for j in range(64):
                    at = c * 2048 + j * 32
                    wide[at : at + 32, :] = rows[j, :32, :].astype(F32)
                    at = c * 512 + j * 8
                    small[at : at + 8, :] = rows[j, 32:, :].astype(F32)

    for ab in range(9):
        for r in range(144):
            q, s = r // 3, r % 3
            out[ab // 3, ab % 3, :, r * Z : (r + 1) * Z] = wide[
                pl.ds(ab * 432 + s * 48 + q, 3, stride=144), :
            ]

    for base, result in ((0, out_one), (288, out_two)):
        picked = [
            jnp.concatenate(
                [small[pl.ds(base + s * 144 + k, 9, stride=16), :] for s in range(2)], axis=1
            )
            for k in range(16)
        ]
        for ab in range(9):
            line = jnp.concatenate([p[:, ab * 24 : (ab + 1) * 24] for p in picked], axis=1)
            for s in range(3):
                lined[s, :9, :] = line[:, s * Z : (s + 1) * Z]
                for k in range(3):
                    at = k * 384 + s * Z
                    result[ab // 3, ab % 3, :, at : at + Z] = lined[
                        s, pl.ds(k, 3, stride=3), :
                    ]
    picked = [
        jnp.concatenate(
            [small[pl.ds(576 + s * CD + k, 12, stride=8), :] for s in range(3)], axis=1
        )
        for k in range(8)
    ]
    for abc in range(8):
        line = jnp.concatenate([p[:, abc * C : (abc + 1) * C] for p in picked], axis=1)
        for k in range(12):
            out_down[abc // 4, abc // 2 % 2, abc % 2 : abc % 2 + 1, k * 384 : (k + 1) * 384] = line[
                k : k + 1, :
            ]


def coarse_grad_kernel(grad_three, coarse_in, out, shifted, left):
    for x in range(2):
        grad = grad_three[x].astype(F32)
        lanes = slice(x * Z, (x + 1) * Z)
        shifted[x, 0] = from_after(grad, Z // 2)
        shifted[x, 1] = grad
        shifted[x, 2] = from_before(grad, Z // 2)
        for c in range(3):
            for r in range(4):
                left[(c * 4 + r) * 48 : (c * 4 + r + 1) * 48, lanes] = shifted[
                    x, c, pl.ds(r, 48, stride=4), :
                ].astype(BF)
    for a in range(3):
        for b in range(3):
            cells = jnp.concatenate(
                [coarse_in[a + x, :, b * Z : (b + 1) * Z] for x in range(2)], axis=1
            )
            part = dot_t(left[...], cells)
            for c in range(3):
                wide = jnp.concatenate(
                    [part[(c * 4 + r) * 48 : (c * 4 + r + 1) * 48, :] for r in range(4)], axis=1
                ).astype(BF)
                tap = (a * 3 + b) * 3 + c
                for s in range(3):
                    at = (tap * 3 + s) * 48
                    out[at : at + 48, :] = wide[:, s * Z : (s + 1) * Z]
    out[81 * 48 :, :] = jnp.zeros((4096 - 81 * 48, Z), BF)


def backward_kernel(
    g_l, g_m, g_r, coarse_hbm, down_hbm, two_hbm, kept_six, kept_eight,
    mid_out, small,
    w_coarse_t, down_own, w_down_t, slope_two, act_one, w_two_t, slope_one, feat_six,
    halves, spread, mid_one, taps, taps_mid, left, sems,
):
    loads = [
        pltpu.make_async_copy(src, dst, sems.at[k])
        for k, (src, dst) in enumerate((
            (coarse_hbm.at[pl.ds(0, 9)], w_coarse_t), (kept_eight.at[pl.ds(8, 2)], down_own),
            (down_hbm, w_down_t), (kept_eight.at[pl.ds(0, 8)], slope_two),
            (kept_six.at[pl.ds(0, 6)], act_one), (two_hbm, w_two_t),
            (kept_six.at[pl.ds(6, 6)], slope_one), (kept_six.at[pl.ds(12, 6)], feat_six),
        ))
    ]
    for load in loads:
        load.start()
    store = pltpu.make_async_copy(mid_one, mid_out, sems.at[8])
    low = low_lanes((CC, Z))

    def prepare(x, carry):
        p0, p1, p2 = g_l[x], g_m[x], g_r[x]
        s0, s1, s2 = swap_halves(p0), swap_halves(p1), swap_halves(p2)
        halves[0, x, :, :Z] = p1
        halves[0, x, :, Z:] = p2
        halves[1, x, :, :Z] = jnp.where(low, s0, s1).astype(BF)
        halves[1, x, :, Z:] = jnp.where(low, s1, s2).astype(BF)
        halves[2, x, :, :Z] = p0
        halves[2, x, :, Z:] = p1
        return carry

    lax.fori_loop(0, 6, prepare, 0)

    row = lax.broadcasted_iota(jnp.int32, (Z, 4 * Z), 0)
    col = lax.broadcasted_iota(jnp.int32, (Z, 4 * Z), 1)
    same = row // (Z // 2) == col // (2 * Z)
    place = jnp.where(same & (col % Z == 2 * (row % (Z // 2)) + (col // Z) % 2), 1.0, 0.0).astype(BF)
    low_down = low_lanes((CD, Z))

    for load in loads[:4]:
        load.wait()
    grad_down = jnp.zeros((CD, 8 * C), F32)
    for x in range(4):
        total = jnp.zeros((3 * CD, 2 * Z), F32)
        for a in range(3):
            for b in range(3):
                total = total + dot(w_coarse_t[a * 3 + b], halves[b, x + 2 - a])
        back = [tap_sum(total, k, CD, Z // 2, True).astype(BF) for k in range(2)]
        if x == 1 or x == 2:
            own = jnp.where(low_down, swap_halves(back[0]), swap_halves(back[1])).astype(BF)
            grad_down = grad_down + dot_t(own, down_own[x - 1])
        for k in range(2):
            wide = dot(back[k], place).astype(BF)
            for y in range(2):
                for c in range(2):
                    spread[c * CD : (c + 1) * CD, (k * 2 + y) * Z : (k * 2 + y + 1) * Z] = wide[
                        :, (y * 2 + c) * Z : (y * 2 + c + 1) * Z
                    ]
        fine = dot(w_down_t[...], spread[...])
        for a in range(2):
            for b in range(2):
                for y in range(4):
                    rows = slice((2 * y + b) * C, (2 * y + b + 1) * C)
                    part = fine[(a * 2 + b) * C : (a * 2 + b + 1) * C, y * Z : (y + 1) * Z]
                    mid = (part * slope_two[2 * x + a, rows, :].astype(F32)).astype(BF)
                    put_back(taps_mid, 2 * x + a, mid, 2 * y + b, 6)
                    if 0 < x < 3 and 0 < y < 3:
                        put_left(left, 2 * x + a - 2, 2 * y + b - 2, mid)
    for s in range(3):
        small[576 + s * CD : 576 + (s + 1) * CD, :] = grad_down[:, s * Z : (s + 1) * Z].astype(BF)

    small[864:, :] = jnp.zeros((1024 - 864, Z), BF)

    def kernel_grad(field, at):
        for x in range(6):
            for y in range(6):
                put(taps, x, field[x, y * C : (y + 1) * C, :], y, 4)
        part = jnp.zeros((3 * C, 9 * C), F32)
        for x in range(4):
            part = part + dot_t(left[x], taps[x * 3 * C : (x + 3) * 3 * C, :])
        row = lax.broadcasted_iota(jnp.int32, part.shape, 0)
        col = lax.broadcasted_iota(jnp.int32, part.shape, 1)
        part = jnp.where((row % C) // 24 == (col % C) // 24, part, 0.0).astype(BF)
        row = lax.broadcasted_iota(jnp.int32, (432, 256), 0)
        col = lax.broadcasted_iota(jnp.int32, (432, 256), 1)
        fold = jnp.where((row // C == col // 24) & (row % 24 == col % 24), 1.0, 0.0).astype(BF)
        part = dot(part, fold).astype(BF)
        for s in range(2):
            small[at + s * 144 : at + (s + 1) * 144, :] = part[:, s * Z : (s + 1) * Z]

    loads[4].wait()
    kernel_grad(act_one, 288)

    loads[5].wait()
    loads[6].wait()

    def step_two(x, carry):
        prod = dot(w_two_t[...], taps_mid[pl.ds(pl.multiple_of(x * 3 * C, 16), 9 * C), :])
        for y in range(6):
            rows = slice(y * C, (y + 1) * C)
            grad = tap_sum(prod, y, C, Z, True)
            mid = (grad * slope_one[x, rows, :].astype(F32)).astype(BF)
            mid_one[x, rows, :] = mid
        return carry

    lax.fori_loop(0, 6, step_two, 0, unroll=3)

    store.start()
    for x in range(4):
        for y in range(4):
            put_left(left, x, y, mid_one[x + 1, (y + 1) * C : (y + 2) * C, :])
    loads[7].wait()
    kernel_grad(feat_six, 0)
    store.wait()


def input_kernel(mid_one, w_one_t, grad_input, taps):
    for x in range(6):
        for y in range(6):
            put_back(taps, x, mid_one[x, y * C : (y + 1) * C, :], y, 4)
    for x in range(4):
        prod = dot(w_one_t[...], taps[x * 3 * C : (x + 3) * 3 * C, :])
        for y in range(4):
            grad_input[x, y * C : (y + 1) * C, :] = tap_sum(prod, y, C, Z, True).astype(BF)


def call(kernel, outs, scratch, n_smem, flops, *args, far_in=(), far_out=(), limit=20):
    vmem = pl.BlockSpec(memory_space=pltpu.VMEM)
    hbm = pl.BlockSpec(memory_space=pltpu.HBM)
    smem = pl.BlockSpec(memory_space=pltpu.SMEM)
    moved = sum(a.size * a.dtype.itemsize for a in args) + sum(
        o.size * o.dtype.itemsize for o in outs
    )
    return pl.pallas_call(
        kernel,
        out_shape=outs,
        in_specs=[
            smem if k < n_smem else hbm if k in far_in else vmem for k in range(len(args))
        ],
        out_specs=[hbm if k in far_out else vmem for k in range(len(outs))],
        scratch_shapes=scratch,
        compiler_params=pltpu.CompilerParams(vmem_limit_bytes=limit * 1024 * 1024),
        cost_estimate=pl.CostEstimate(flops=flops, bytes_accessed=moved, transcendentals=0),
    )(*args)


def shape(dims, dtype=BF):
    return jax.ShapeDtypeStruct(dims, dtype)


def neighbours(array, axis):
    size = lax.axis_size(axis)
    up = [(i, i + 1) for i in range(size - 1)]
    down = [(j, i) for i, j in up]
    return lax.ppermute(array, axis, up), lax.ppermute(array, axis, down)


def other_core(array):
    return lax.ppermute(array, "core", [(0, 1), (1, 0)])


def pair_sum(parts, core):
    half = parts.shape[0] // 2
    keep = lax.dynamic_slice_in_dim(parts, core * half, half, 0)
    send = lax.dynamic_slice_in_dim(parts, (1 - core) * half, half, 0)
    both = keep.astype(F32) + other_core(send).astype(F32)
    return both.astype(BF).reshape(64, half // 64, Z)


def per_device(features, conv_one, conv_two, down_weight, coarse_weight, cotangent):
    gx, gy, core = lax.axis_index("gx"), lax.axis_index(GY), lax.axis_index("core")
    last_x, last_y = lax.axis_size("gx") - 1, lax.axis_size(GY) - 1
    flags = jnp.stack([gx > 0, gx < last_x, gy > 0, gy < last_y]).astype(F32)

    feat = jnp.transpose(features, (1, 2, 0, 3)).reshape(4, 4 * C, Z)
    before, after = neighbours(feat, "gx")
    one = conv_one.reshape(27, C, C // 2)
    two = conv_two.reshape(27, C, C // 2)
    down = down_weight.reshape(8, CD, C)
    w_coarse = coarse_weight.reshape(9, 3 * CC, CD)
    before, after, one, two, down, w_coarse = lax.optimization_barrier(
        (before, after, one, two, down, w_coarse)
    )
    feat = jnp.concatenate([before, feat, after], axis=0)
    cot = jnp.transpose(cotangent.reshape(12, 16, 2, Z), (1, 0, 2, 3)).astype(BF)
    feat, cot = lax.optimization_barrier((feat, cot))
    feat_l, feat_r = neighbours(feat, GY)
    cot = lax.all_to_all(cot, "gx", 0, 0, tiled=True)

    kept_six, kept_eight, coarse_in = call(
        fine_kernel,
        [shape((400, 6 * C, Z)), shape((300, 8 * C, Z)), shape((4, CD, 3 * Z))],
        [
            pltpu.VMEM((144, 432), BF), pltpu.VMEM((144, 432), BF), pltpu.VMEM((CD, 8 * C), BF),
            pltpu.VMEM((36 * C, 10 * Z), BF), pltpu.VMEM((30 * C, 8 * Z), BF),
            pltpu.VMEM((10, 6 * C, Z), BF), pltpu.VMEM((6 * C, 2 * Z), BF), pltpu.VMEM((4, 8 * C, 3 * Z), BF),
            pltpu.VMEM((10, 6 * C, Z), BF), pltpu.VMEM((8, 8 * C, Z), BF),
            pltpu.SemaphoreType.DMA((7,)),
        ],
        1, 16_000_000_000,
        flags, feat_l, feat, feat_r, one, two, down, far_out=range(2), limit=40,
    )
    coarse_in, cot = lax.optimization_barrier((coarse_in, cot))
    cot = jnp.transpose(cot.reshape(CC, 2, Z), (1, 0, 2))
    coarse_out, grad_three = call(
        coarse_kernel, [shape((2, CC, Z)), shape((2, CC, Z))], [], 0, 300_000_000,
        coarse_in, w_coarse, cot,
    )

    before, after = neighbours(grad_three, "gx")
    grad_three, one, two, down, w_coarse = lax.optimization_barrier(
        (grad_three, one, two, down, w_coarse)
    )
    backs = [shape((144, 432)), shape((144, 432)), shape((4 * C, 2 * CD)), shape((200, 3 * CD, CC))]
    w_one_t, w_two_t, w_down_t, w_coarse_t = call(
        back_kernel, backs,
        [pltpu.VMEM(w.shape, BF) for w in backs[:3]]
        + [pltpu.VMEM((9, 3 * CD, CC), BF), pltpu.SemaphoreType.DMA((4,))], 0, 0,
        one, two, down, w_coarse, far_out=range(4), limit=40,
    )
    before, after, w_one_t, w_two_t, w_down_t, w_coarse_t = lax.optimization_barrier(
        (before, after, w_one_t, w_two_t, w_down_t, w_coarse_t)
    )
    wide = jnp.concatenate([before, grad_three, after], axis=0)
    g_l, g_r = neighbours(wide, GY)
    wide, grad_own = lax.optimization_barrier((wide, grad_three))
    (coarse_part,) = call(
        coarse_grad_kernel,
        [shape((4096, Z))],
        [pltpu.VMEM((2, 3, CC, Z), F32), pltpu.VMEM((3 * CC, 2 * Z), BF)],
        0, 500_000_000,
        grad_own, coarse_in,
    )
    g_l, g_r, coarse_part = lax.optimization_barrier((g_l, g_r, coarse_part))
    coarse_mine = pair_sum(coarse_part, core)
    slots = jnp.transpose(coarse_out.reshape(2, 16, 12, Z), (1, 0, 2, 3)).reshape(16, 1, 24, Z)
    there = lax.broadcasted_iota(jnp.int32, (16, 4, 24, Z), 1) == lax.axis_index("x")
    slots = jnp.where(there, slots, jnp.zeros((), BF)).reshape(64, 24, Z)

    mid_one, small = call(
        backward_kernel,
        [shape((6, 6 * C, Z)), shape((1024, Z))],
        [
            pltpu.VMEM((9, 3 * CD, CC), BF), pltpu.VMEM((2, 8 * C, Z), BF),
            pltpu.VMEM((4 * C, 2 * CD), BF), pltpu.VMEM((8, 8 * C, Z), BF),
            pltpu.VMEM((6, 6 * C, Z), BF), pltpu.VMEM((144, 432), BF),
            pltpu.VMEM((6, 6 * C, Z), BF), pltpu.VMEM((6, 6 * C, Z), BF),
            pltpu.VMEM((3, 6, CC, 2 * Z), BF), pltpu.VMEM((2 * CD, 4 * Z), BF),
            pltpu.VMEM((6, 6 * C, Z), BF), pltpu.VMEM((18 * C, 4 * Z), BF),
            pltpu.VMEM((24 * C, 6 * Z), BF), pltpu.VMEM((4, 3 * C, 4 * Z), BF),
            pltpu.SemaphoreType.DMA((9,)),
        ],
        0, 12_000_000_000,
        g_l, wide, g_r, w_coarse_t, w_down_t, w_two_t, kept_six, kept_eight,
        far_in=range(3, 8), far_out=(0,), limit=40,
    )
    small, coarse_mine, slots = lax.optimization_barrier((small, coarse_mine, slots))
    parts = jnp.concatenate([coarse_mine, pair_sum(small, core), slots], axis=1)
    parts = lax.all_to_all(parts, SAME_CORE, 0, 0, tiled=True)
    out = lax.dynamic_index_in_dim(
        parts[:, 40:].reshape(16, 4, 24, Z), lax.axis_index("x"), 1, keepdims=False
    )
    mine = jnp.sum(parts[:, :40].astype(F32), axis=0).astype(BF)
    (grad_input,) = call(
        input_kernel, [shape((4, 4 * C, Z))], [pltpu.VMEM((18 * C, 4 * Z), BF)], 0, 1_000_000_000,
        mid_one, w_one_t,
    )
    got = lax.all_to_all(
        jnp.broadcast_to(mine[None], (64,) + mine.shape), SAME_CORE, 0, 0, tiled=True
    )
    other = other_core(got)
    out = jnp.transpose(out.reshape(32, 12, Z), (1, 0, 2))
    grad_input = jnp.transpose(grad_input.reshape(4, 4, C, Z), (2, 0, 1, 3))

    grad_coarse, grad_one, grad_two, grad_down = call(
        final_kernel,
        [
            shape((3, 3, 3, CC * CD), F32), shape((3, 3, 3, C * 24), F32),
            shape((3, 3, 3, C * 24), F32), shape((2, 2, 2, CD * C), F32),
        ],
        [pltpu.VMEM((4096, Z), F32), pltpu.VMEM((1024, Z), F32), pltpu.VMEM((3, 16, Z), F32)],
        1, 0,
        core.astype(jnp.int32).reshape(1), got, other,
    )
    return out, grad_input, grad_one, grad_two, grad_down, grad_coarse


def solution(mesh):
    whole = jax.sharding.Mesh(mesh.devices.reshape(16, 4, 2), ("gx", "x", "core"))
    fine, coarse = P(None, "gx", GY, None), P("gx", None, GY)
    return jax.shard_map(
        per_device,
        mesh=whole,
        in_specs=(fine, P(), P(), P(), P(), coarse),
        out_specs=(coarse, fine, P(), P(), P(), P()),
        check_vma=False,
    )
```

```python
import jax
import jax.numpy as jnp
from jax import lax
from jax.experimental import pallas as pl
from jax.experimental.pallas import tpu as pltpu
from jax.sharding import PartitionSpec as P

BF = jnp.bfloat16
F32 = jnp.float32
C = 48
CD = 96
CC = 192
Z = 128
GY = ("x", "core")
ALL = ("gx", "x", "core")
SAME_CORE = ("gx", "x")


def dot(a, b):
    return jnp.dot(a, b, preferred_element_type=F32)


def dot_t(a, b):
    return lax.dot_general(a, b, (((1,), (1,)), ((), ())), preferred_element_type=F32)


def sigmoid(v):
    return 0.5 * jnp.tanh(0.5 * v) + 0.5


def from_before(v, segment):
    lane = lax.broadcasted_iota(jnp.int32, v.shape, 1)
    return jnp.where(lane % segment == 0, 0.0, pltpu.roll(v, 1, 1))


def from_after(v, segment):
    lane = lax.broadcasted_iota(jnp.int32, v.shape, 1)
    return jnp.where(lane % segment == segment - 1, 0.0, pltpu.roll(v, Z - 1, 1))


def tap_sum(y, lanes, rows, segment, flipped):
    one, two, three = (y[k * rows : (k + 1) * rows, lanes * Z : (lanes + 1) * Z] for k in range(3))
    if flipped:
        return from_after(one, segment) + two + from_before(three, segment)
    return from_before(one, segment) + two + from_after(three, segment)


def swap_halves(v):
    return pltpu.roll(v.astype(F32), Z // 2, 1)


def low_lanes(shape):
    return lax.broadcasted_iota(jnp.int32, shape, 1) < Z // 2


def put(taps, x, piece, y, count):
    for b in range(3):
        if 0 <= y - b < count:
            at = x * (3 * C) + b * C
            if not isinstance(x, int):
                at = pl.multiple_of(at, 16)
            taps[pl.ds(at, C), (y - b) * Z : (y - b + 1) * Z] = piece


def put_back(taps, x, piece, y, count):
    for b in range(3):
        if 0 <= y - 2 + b < count:
            at = x * (3 * C) + b * C
            if not isinstance(x, int):
                at = pl.multiple_of(at, 16)
            taps[pl.ds(at, C), (y - 2 + b) * Z : (y - 1 + b) * Z] = piece


def put_left(left, x, y, grad):
    lanes = slice(y * Z, (y + 1) * Z)
    wide = grad.astype(F32)
    left[x, :C, lanes] = from_after(wide, Z).astype(BF)
    left[x, C : 2 * C, lanes] = grad
    left[x, 2 * C :, lanes] = from_before(wide, Z).astype(BF)


def fine_kernel(
    flags, feat_l, feat_m, feat_r, one, two, down,
    kept_six, kept_eight, coarse_in,
    w_one, w_two, w_down, taps_one, taps_two, act_v, rows_two, down_all, slope_a, slope_b, sems,
):
    feats = (feat_l, feat_m, feat_r)
    inner = pl.ds(3, 6)
    copies = [
        pltpu.make_async_copy(
            feat_l.at[inner, pl.ds(3 * C, C), :], kept_six.at[pl.ds(12, 6), pl.ds(0, C), :], sems.at[0]
        ),
        pltpu.make_async_copy(
            feat_m.at[inner], kept_six.at[pl.ds(12, 6), pl.ds(C, 4 * C), :], sems.at[1]
        ),
        pltpu.make_async_copy(
            feat_r.at[inner, pl.ds(0, C), :], kept_six.at[pl.ds(12, 6), pl.ds(5 * C, C), :], sems.at[2]
        ),
        pltpu.make_async_copy(
            act_v.at[pl.ds(2, 6)], kept_six.at[pl.ds(0, 6)], sems.at[3]
        ),
        pltpu.make_async_copy(
            slope_a.at[pl.ds(2, 6)], kept_six.at[pl.ds(6, 6)], sems.at[4]
        ),
        pltpu.make_async_copy(slope_b, kept_eight.at[pl.ds(0, 8)], sems.at[5]),
        pltpu.make_async_copy(
            down_all.at[pl.ds(1, 2), :, pl.ds(Z, Z)], kept_eight.at[pl.ds(8, 2)], sems.at[6]
        ),
    ]
    for copy in copies[:3]:
        copy.start()
    for taps, w in ((one, w_one), (two, w_two)):
        for c in range(3):
            w[c * C : (c + 1) * C, :] = grouped(taps, c).astype(BF)
    w_down[...] = jnp.concatenate([down[k].astype(F32) for k in range(8)], axis=1).astype(BF)

    def valid(x, lo, hi):
        ok_l = jnp.where(x < lo, flags[0], 1.0)
        return jnp.where(x >= hi, flags[1], ok_l)

    def valid_y(y, lo, hi):
        if y < lo:
            return flags[2]
        if y >= hi:
            return flags[3]
        return 1.0

    def spread_one(x, carry):
        for y in range(12):
            piece = feats[y // 4][x, (y % 4) * C : (y % 4 + 1) * C, :]
            put(taps_one, x, piece, y, 10)
        return carry

    lax.fori_loop(0, 12, spread_one, 0, unroll=4)

    def step_one(x, carry):
        prod = dot(w_one[...], taps_one[pl.ds(pl.multiple_of(x * 3 * C, 16), 9 * C), :])
        ok_x = valid(x, 3, 7)
        for y in range(10):
            pre = tap_sum(prod, y, C, Z, False)
            sig = sigmoid(pre)
            ok = ok_x * valid_y(y, 3, 7)
            act = (pre * sig * ok).astype(BF)
            put(taps_two, x, act, y, 8)
            if 2 <= y < 8:
                slp = (sig * (1.0 + pre * (1.0 - sig)) * ok).astype(BF)

                act_v[x, (y - 2) * C : (y - 1) * C, :] = act
                slope_a[x, (y - 2) * C : (y - 1) * C, :] = slp
        return carry

    lax.fori_loop(0, 10, step_one, 0, unroll=10)
    copies[3].start()
    copies[4].start()

    row = lax.broadcasted_iota(jnp.int32, (2 * Z, 2 * Z), 0)
    col = lax.broadcasted_iota(jnp.int32, (2 * Z, 2 * Z), 1)
    same = (row // Z) == (col % Z) // (Z // 2)
    select = jnp.where(same & (row % Z == 2 * (col % (Z // 2)) + col // Z), 1.0, 0.0).astype(BF)

    def step_two(x, carry):
        prod = dot(w_two[...], taps_two[pl.ds(pl.multiple_of(x * 3 * C, 16), 9 * C), :])
        ok_x = valid(x, 2, 6)
        for y in range(8):
            pre = tap_sum(prod, y, C, Z, False)
            sig = sigmoid(pre)
            ok = ok_x * valid_y(y, 2, 6)
            act = (pre * sig * ok).astype(BF)
            slope_b[x, y * C : (y + 1) * C, :] = (sig * (1.0 + pre * (1.0 - sig)) * ok).astype(BF)
            pair, b = y // 2, y % 2
            if pair < 3:
                rows_two[(pair * 2 + b) * C : (pair * 2 + b + 1) * C, :Z] = act
            if pair > 0:
                rows_two[((pair - 1) * 2 + b) * C : ((pair - 1) * 2 + b + 1) * C, Z:] = act
        picked = dot(rows_two[...], select).astype(BF)
        a = x % 2
        for pair in range(3):
            for b in range(2):
                for c in range(2):
                    at = pl.multiple_of(a * (4 * C) + (b * 2 + c) * C, 16)
                    down_all[x // 2, pl.ds(at, C), pair * Z : (pair + 1) * Z] = picked[
                        (pair * 2 + b) * C : (pair * 2 + b + 1) * C, c * Z : (c + 1) * Z
                    ]
        return carry

    lax.fori_loop(0, 8, step_two, 0, unroll=8)
    copies[5].start()
    copies[6].start()
    for x in range(4):
        coarse_in[x] = dot(w_down[...], down_all[x]).astype(BF)
    for copy in copies:
        copy.wait()


def coarse_kernel(coarse_in, w_coarse, cot, coarse_out, grad_three):
    total = jnp.zeros((3 * CC, 2 * Z), F32)
    for a in range(3):
        for b in range(3):
            cells = jnp.concatenate(
                [coarse_in[a + x, :, b * Z : (b + 1) * Z] for x in range(2)], axis=1
            )
            total = total + dot(w_coarse[a * 3 + b], cells)
    for x in range(2):
        pre = tap_sum(total, x, CC, Z // 2, False)
        sig = sigmoid(pre)
        coarse_out[x] = (pre * sig).astype(BF)
        grad_three[x] = (cot[x].astype(F32) * (sig * (1.0 + pre * (1.0 - sig)))).astype(BF)


def grouped(taps, c):
    first = lax.broadcasted_iota(jnp.int32, (C, C // 2), 0) < C // 2
    parts = []
    for ab in range(9):
        tap = taps[ab * 3 + c].astype(F32)
        parts += [jnp.where(first, tap, 0.0), jnp.where(first, 0.0, tap)]
    return jnp.concatenate(parts, axis=1)


def back_kernel(one, two, down, coarse, one_out, two_out, down_out, coarse_out,
                w_one_t, w_two_t, w_down_t, w_coarse_t, sems):
    copies = [
        pltpu.make_async_copy(src, dst, sems.at[k])
        for k, (src, dst) in enumerate((
            (w_one_t, one_out), (w_two_t, two_out), (w_down_t, down_out), (w_coarse_t, coarse_out.at[pl.ds(0, 9)])
        ))
    ]
    for taps, out in ((one, w_one_t), (two, w_two_t)):
        for c in range(3):
            turned = grouped(taps, c).T
            out[c * C : (c + 1) * C, :] = jnp.concatenate(
                [
                    turned[ab * C : (ab + 1) * C, :]
                    for ab in (6, 7, 8, 3, 4, 5, 0, 1, 2)
                ],
                axis=1,
            ).astype(BF)
    for ab in range(4):
        w_down_t[ab * C : (ab + 1) * C, :] = jnp.concatenate(
            [down[ab * 2 + c].astype(F32).T for c in range(2)], axis=1
        ).astype(BF)

    def turn(ab, carry):
        for c in range(3):
            w_coarse_t[ab, c * CD : (c + 1) * CD, :] = (
                coarse[ab, c * CC : (c + 1) * CC, :].astype(F32).T.astype(BF)
            )
        return carry

    for copy in copies[:3]:
        copy.start()
    lax.fori_loop(0, 9, turn, 0, unroll=3)
    copies[3].start()
    for copy in copies:
        copy.wait()


def final_kernel(core, got, other, out, out_one, out_two, out_down, wide, small, lined):
    for c in range(2):
        for mine, rows in ((True, got), (False, other)):

            @pl.when((core[0] == c) == mine)
            def _():
                for j in range(64):
                    at = c * 2048 + j * 32
                    wide[at : at + 32, :] = rows[j, :32, :].astype(F32)
                    at = c * 512 + j * 8
                    small[at : at + 8, :] = rows[j, 32:, :].astype(F32)

    for ab in range(9):
        for r in range(144):
            q, s = r // 3, r % 3
            out[ab // 3, ab % 3, :, r * Z : (r + 1) * Z] = wide[
                pl.ds(ab * 432 + s * 48 + q, 3, stride=144), :
            ]

    for base, result in ((0, out_one), (288, out_two)):
        picked = [
            jnp.concatenate(
                [small[pl.ds(base + s * 144 + k, 9, stride=16), :] for s in range(2)], axis=1
            )
            for k in range(16)
        ]
        for ab in range(9):
            line = jnp.concatenate([p[:, ab * 24 : (ab + 1) * 24] for p in picked], axis=1)
            for s in range(3):
                lined[s, :9, :] = line[:, s * Z : (s + 1) * Z]
                for k in range(3):
                    at = k * 384 + s * Z
                    result[ab // 3, ab % 3, :, at : at + Z] = lined[
                        s, pl.ds(k, 3, stride=3), :
                    ]
    picked = [
        jnp.concatenate(
            [small[pl.ds(576 + s * CD + k, 12, stride=8), :] for s in range(3)], axis=1
        )
        for k in range(8)
    ]
    for abc in range(8):
        line = jnp.concatenate([p[:, abc * C : (abc + 1) * C] for p in picked], axis=1)
        for k in range(12):
            out_down[abc // 4, abc // 2 % 2, abc % 2 : abc % 2 + 1, k * 384 : (k + 1) * 384] = line[
                k : k + 1, :
            ]


def coarse_grad_kernel(grad_three, coarse_in, out, shifted, left):
    for x in range(2):
        grad = grad_three[x].astype(F32)
        lanes = slice(x * Z, (x + 1) * Z)
        shifted[x, 0] = from_after(grad, Z // 2)
        shifted[x, 1] = grad
        shifted[x, 2] = from_before(grad, Z // 2)
        for c in range(3):
            for r in range(4):
                left[(c * 4 + r) * 48 : (c * 4 + r + 1) * 48, lanes] = shifted[
                    x, c, pl.ds(r, 48, stride=4), :
                ].astype(BF)
    for a in range(3):
        for b in range(3):
            cells = jnp.concatenate(
                [coarse_in[a + x, :, b * Z : (b + 1) * Z] for x in range(2)], axis=1
            )
            part = dot_t(left[...], cells)
            for c in range(3):
                wide = jnp.concatenate(
                    [part[(c * 4 + r) * 48 : (c * 4 + r + 1) * 48, :] for r in range(4)], axis=1
                ).astype(BF)
                tap = (a * 3 + b) * 3 + c
                for s in range(3):
                    at = (tap * 3 + s) * 48
                    out[at : at + 48, :] = wide[:, s * Z : (s + 1) * Z]
    out[81 * 48 :, :] = jnp.zeros((4096 - 81 * 48, Z), BF)


def backward_kernel(
    g_l, g_m, g_r, coarse_hbm, down_hbm, two_hbm, kept_six, kept_eight,
    mid_out, small,
    w_coarse_t, down_own, w_down_t, slope_two, act_one, w_two_t, slope_one, feat_six,
    halves, spread, mid_one, taps, taps_mid, left, sems,
):
    loads = [
        pltpu.make_async_copy(src, dst, sems.at[k])
        for k, (src, dst) in enumerate((
            (coarse_hbm.at[pl.ds(0, 9)], w_coarse_t), (kept_eight.at[pl.ds(8, 2)], down_own),
            (down_hbm, w_down_t), (kept_eight.at[pl.ds(0, 8)], slope_two),
            (kept_six.at[pl.ds(0, 6)], act_one), (two_hbm, w_two_t),
            (kept_six.at[pl.ds(6, 6)], slope_one), (kept_six.at[pl.ds(12, 6)], feat_six),
        ))
    ]
    for load in loads:
        load.start()
    store = pltpu.make_async_copy(mid_one, mid_out, sems.at[8])
    low = low_lanes((CC, Z))

    def prepare(x, carry):
        p0, p1, p2 = g_l[x], g_m[x], g_r[x]
        s0, s1, s2 = swap_halves(p0), swap_halves(p1), swap_halves(p2)
        halves[0, x, :, :Z] = p1
        halves[0, x, :, Z:] = p2
        halves[1, x, :, :Z] = jnp.where(low, s0, s1).astype(BF)
        halves[1, x, :, Z:] = jnp.where(low, s1, s2).astype(BF)
        halves[2, x, :, :Z] = p0
        halves[2, x, :, Z:] = p1
        return carry

    lax.fori_loop(0, 6, prepare, 0)

    row = lax.broadcasted_iota(jnp.int32, (Z, 4 * Z), 0)
    col = lax.broadcasted_iota(jnp.int32, (Z, 4 * Z), 1)
    same = row // (Z // 2) == col // (2 * Z)
    place = jnp.where(same & (col % Z == 2 * (row % (Z // 2)) + (col // Z) % 2), 1.0, 0.0).astype(BF)
    low_down = low_lanes((CD, Z))

    for load in loads[:4]:
        load.wait()
    grad_down = jnp.zeros((CD, 8 * C), F32)
    for x in range(4):
        total = jnp.zeros((3 * CD, 2 * Z), F32)
        for a in range(3):
            for b in range(3):
                total = total + dot(w_coarse_t[a * 3 + b], halves[b, x + 2 - a])
        back = [tap_sum(total, k, CD, Z // 2, True).astype(BF) for k in range(2)]
        if x == 1 or x == 2:
            own = jnp.where(low_down, swap_halves(back[0]), swap_halves(back[1])).astype(BF)
            grad_down = grad_down + dot_t(own, down_own[x - 1])
        for k in range(2):
            wide = dot(back[k], place).astype(BF)
            for y in range(2):
                for c in range(2):
                    spread[c * CD : (c + 1) * CD, (k * 2 + y) * Z : (k * 2 + y + 1) * Z] = wide[
                        :, (y * 2 + c) * Z : (y * 2 + c + 1) * Z
                    ]
        fine = dot(w_down_t[...], spread[...])
        for a in range(2):
            for b in range(2):
                for y in range(4):
                    rows = slice((2 * y + b) * C, (2 * y + b + 1) * C)
                    part = fine[(a * 2 + b) * C : (a * 2 + b + 1) * C, y * Z : (y + 1) * Z]
                    mid = (part * slope_two[2 * x + a, rows, :].astype(F32)).astype(BF)
                    put_back(taps_mid, 2 * x + a, mid, 2 * y + b, 6)
                    if 0 < x < 3 and 0 < y < 3:
                        put_left(left, 2 * x + a - 2, 2 * y + b - 2, mid)
    for s in range(3):
        small[576 + s * CD : 576 + (s + 1) * CD, :] = grad_down[:, s * Z : (s + 1) * Z].astype(BF)

    small[864:, :] = jnp.zeros((1024 - 864, Z), BF)

    def kernel_grad(field, at):
        for x in range(6):
            for y in range(6):
                put(taps, x, field[x, y * C : (y + 1) * C, :], y, 4)
        part = jnp.zeros((3 * C, 9 * C), F32)
        for x in range(4):
            part = part + dot_t(left[x], taps[x * 3 * C : (x + 3) * 3 * C, :])
        row = lax.broadcasted_iota(jnp.int32, part.shape, 0)
        col = lax.broadcasted_iota(jnp.int32, part.shape, 1)
        part = jnp.where((row % C) // 24 == (col % C) // 24, part, 0.0).astype(BF)
        row = lax.broadcasted_iota(jnp.int32, (432, 256), 0)
        col = lax.broadcasted_iota(jnp.int32, (432, 256), 1)
        fold = jnp.where((row // C == col // 24) & (row % 24 == col % 24), 1.0, 0.0).astype(BF)
        part = dot(part, fold).astype(BF)
        for s in range(2):
            small[at + s * 144 : at + (s + 1) * 144, :] = part[:, s * Z : (s + 1) * Z]

    loads[4].wait()
    kernel_grad(act_one, 288)

    loads[5].wait()
    loads[6].wait()

    def step_two(x, carry):
        prod = dot(w_two_t[...], taps_mid[pl.ds(pl.multiple_of(x * 3 * C, 16), 9 * C), :])
        for y in range(6):
            rows = slice(y * C, (y + 1) * C)
            grad = tap_sum(prod, y, C, Z, True)
            mid = (grad * slope_one[x, rows, :].astype(F32)).astype(BF)
            mid_one[x, rows, :] = mid
        return carry

    lax.fori_loop(0, 6, step_two, 0, unroll=6)

    store.start()
    for x in range(4):
        for y in range(4):
            put_left(left, x, y, mid_one[x + 1, (y + 1) * C : (y + 2) * C, :])
    loads[7].wait()
    kernel_grad(feat_six, 0)
    store.wait()


def input_kernel(mid_one, w_one_t, grad_input, taps):
    for x in range(6):
        for y in range(6):
            put_back(taps, x, mid_one[x, y * C : (y + 1) * C, :], y, 4)
    for x in range(4):
        prod = dot(w_one_t[...], taps[x * 3 * C : (x + 3) * 3 * C, :])
        for y in range(4):
            grad_input[x, y * C : (y + 1) * C, :] = tap_sum(prod, y, C, Z, True).astype(BF)


def call(kernel, outs, scratch, n_smem, flops, *args, far_in=(), far_out=(), limit=20):
    vmem = pl.BlockSpec(memory_space=pltpu.VMEM)
    hbm = pl.BlockSpec(memory_space=pltpu.HBM)
    smem = pl.BlockSpec(memory_space=pltpu.SMEM)
    moved = sum(a.size * a.dtype.itemsize for a in args) + sum(
        o.size * o.dtype.itemsize for o in outs
    )
    return pl.pallas_call(
        kernel,
        out_shape=outs,
        in_specs=[
            smem if k < n_smem else hbm if k in far_in else vmem for k in range(len(args))
        ],
        out_specs=[hbm if k in far_out else vmem for k in range(len(outs))],
        scratch_shapes=scratch,
        compiler_params=pltpu.CompilerParams(vmem_limit_bytes=limit * 1024 * 1024),
        cost_estimate=pl.CostEstimate(flops=flops, bytes_accessed=moved, transcendentals=0),
    )(*args)


def shape(dims, dtype=BF):
    return jax.ShapeDtypeStruct(dims, dtype)


def neighbours(array, axis):
    size = lax.axis_size(axis)
    up = [(i, i + 1) for i in range(size - 1)]
    down = [(j, i) for i, j in up]
    return lax.ppermute(array, axis, up), lax.ppermute(array, axis, down)


def other_core(array):
    return lax.ppermute(array, "core", [(0, 1), (1, 0)])


def pair_sum(parts, core, kept=None):
    half = parts.shape[0] // 2
    keep = lax.dynamic_slice_in_dim(parts if kept is None else kept, core * half, half, 0)
    send = lax.dynamic_slice_in_dim(parts, (1 - core) * half, half, 0)
    both = keep.astype(F32) + other_core(send).astype(F32)
    return both.astype(BF).reshape(64, half // 64, Z)


def per_device(features, conv_one, conv_two, down_weight, coarse_weight, cotangent):
    gx, gy, core = lax.axis_index("gx"), lax.axis_index(GY), lax.axis_index("core")
    last_x, last_y = lax.axis_size("gx") - 1, lax.axis_size(GY) - 1
    flags = jnp.stack([gx > 0, gx < last_x, gy > 0, gy < last_y]).astype(F32)

    feat = jnp.transpose(features, (1, 2, 0, 3)).reshape(4, 4 * C, Z)
    before, after = neighbours(feat, "gx")
    one = conv_one.reshape(27, C, C // 2)
    two = conv_two.reshape(27, C, C // 2)
    down = down_weight.reshape(8, CD, C)
    w_coarse = coarse_weight.reshape(9, 3 * CC, CD)
    before, after, one, two, down, w_coarse = lax.optimization_barrier(
        (before, after, one, two, down, w_coarse)
    )
    feat = jnp.concatenate([before, feat, after], axis=0)
    cot = jnp.transpose(cotangent.reshape(12, 16, 2, Z), (1, 0, 2, 3)).astype(BF)
    feat, cot = lax.optimization_barrier((feat, cot))
    feat_l, feat_r = neighbours(feat, GY)
    cot = lax.all_to_all(cot, "gx", 0, 0, tiled=True)

    kept_six, kept_eight, coarse_in = call(
        fine_kernel,
        [shape((400, 6 * C, Z)), shape((300, 8 * C, Z)), shape((4, CD, 3 * Z))],
        [
            pltpu.VMEM((144, 432), BF), pltpu.VMEM((144, 432), BF), pltpu.VMEM((CD, 8 * C), BF),
            pltpu.VMEM((36 * C, 10 * Z), BF), pltpu.VMEM((30 * C, 8 * Z), BF),
            pltpu.VMEM((10, 6 * C, Z), BF), pltpu.VMEM((6 * C, 2 * Z), BF), pltpu.VMEM((4, 8 * C, 3 * Z), BF),
            pltpu.VMEM((10, 6 * C, Z), BF), pltpu.VMEM((8, 8 * C, Z), BF),
            pltpu.SemaphoreType.DMA((7,)),
        ],
        1, 16_000_000_000,
        flags, feat_l, feat, feat_r, one, two, down, far_out=range(2), limit=40,
    )
    coarse_in, cot = lax.optimization_barrier((coarse_in, cot))
    cot = jnp.transpose(cot.reshape(CC, 2, Z), (1, 0, 2))
    coarse_out, grad_three = call(
        coarse_kernel, [shape((2, CC, Z)), shape((2, CC, Z))], [], 0, 300_000_000,
        coarse_in, w_coarse, cot,
    )

    before, after = neighbours(grad_three, "gx")
    grad_three, one, two, down, w_coarse = lax.optimization_barrier(
        (grad_three, one, two, down, w_coarse)
    )
    backs = [shape((144, 432)), shape((144, 432)), shape((4 * C, 2 * CD)), shape((200, 3 * CD, CC))]
    w_one_t, w_two_t, w_down_t, w_coarse_t = call(
        back_kernel, backs,
        [pltpu.VMEM(w.shape, BF) for w in backs[:3]]
        + [pltpu.VMEM((9, 3 * CD, CC), BF), pltpu.SemaphoreType.DMA((4,))], 0, 0,
        one, two, down, w_coarse, far_out=range(4), limit=40,
    )
    before, after, w_one_t, w_two_t, w_down_t, w_coarse_t = lax.optimization_barrier(
        (before, after, w_one_t, w_two_t, w_down_t, w_coarse_t)
    )
    wide = jnp.concatenate([before, grad_three, after], axis=0)
    g_l, g_r = neighbours(wide, GY)
    wide, grad_own = lax.optimization_barrier((wide, grad_three))
    (coarse_part,) = call(
        coarse_grad_kernel,
        [shape((4096, Z))],
        [pltpu.VMEM((2, 3, CC, Z), F32), pltpu.VMEM((3 * CC, 2 * Z), BF)],
        0, 500_000_000,
        grad_own, coarse_in,
    )
    g_l, g_r, kept = lax.optimization_barrier((g_l, g_r, coarse_part))
    coarse_mine = pair_sum(coarse_part, core, kept)
    slots = jnp.transpose(coarse_out.reshape(2, 16, 12, Z), (1, 0, 2, 3)).reshape(16, 1, 24, Z)
    there = lax.broadcasted_iota(jnp.int32, (16, 4, 24, Z), 1) == lax.axis_index("x")
    slots = jnp.where(there, slots, jnp.zeros((), BF)).reshape(64, 24, Z)

    mid_one, small = call(
        backward_kernel,
        [shape((6, 6 * C, Z)), shape((1024, Z))],
        [
            pltpu.VMEM((9, 3 * CD, CC), BF), pltpu.VMEM((2, 8 * C, Z), BF),
            pltpu.VMEM((4 * C, 2 * CD), BF), pltpu.VMEM((8, 8 * C, Z), BF),
            pltpu.VMEM((6, 6 * C, Z), BF), pltpu.VMEM((144, 432), BF),
            pltpu.VMEM((6, 6 * C, Z), BF), pltpu.VMEM((6, 6 * C, Z), BF),
            pltpu.VMEM((3, 6, CC, 2 * Z), BF), pltpu.VMEM((2 * CD, 4 * Z), BF),
            pltpu.VMEM((6, 6 * C, Z), BF), pltpu.VMEM((18 * C, 4 * Z), BF),
            pltpu.VMEM((24 * C, 6 * Z), BF), pltpu.VMEM((4, 3 * C, 4 * Z), BF),
            pltpu.SemaphoreType.DMA((9,)),
        ],
        0, 12_000_000_000,
        g_l, wide, g_r, w_coarse_t, w_down_t, w_two_t, kept_six, kept_eight,
        far_in=range(3, 8), far_out=(0,), limit=40,
    )
    small, coarse_mine, slots = lax.optimization_barrier((small, coarse_mine, slots))
    parts = jnp.concatenate([coarse_mine, pair_sum(small, core), slots], axis=1)
    parts = lax.all_to_all(parts, SAME_CORE, 0, 0, tiled=True)
    out = lax.dynamic_index_in_dim(
        parts[:, 40:].reshape(16, 4, 24, Z), lax.axis_index("x"), 1, keepdims=False
    )
    mine = jnp.sum(parts[:, :40].astype(F32), axis=0).astype(BF)
    (grad_input,) = call(
        input_kernel, [shape((4, 4 * C, Z))], [pltpu.VMEM((18 * C, 4 * Z), BF)], 0, 1_000_000_000,
        mid_one, w_one_t,
    )
    got = lax.all_to_all(
        jnp.broadcast_to(mine[None], (64,) + mine.shape), SAME_CORE, 0, 0, tiled=True
    )
    other = other_core(got)
    out = jnp.transpose(out.reshape(32, 12, Z), (1, 0, 2))
    grad_input = jnp.transpose(grad_input.reshape(4, 4, C, Z), (2, 0, 1, 3))

    grad_coarse, grad_one, grad_two, grad_down = call(
        final_kernel,
        [
            shape((3, 3, 3, CC * CD), F32), shape((3, 3, 3, C * 24), F32),
            shape((3, 3, 3, C * 24), F32), shape((2, 2, 2, CD * C), F32),
        ],
        [pltpu.VMEM((4096, Z), F32), pltpu.VMEM((1024, Z), F32), pltpu.VMEM((3, 16, Z), F32)],
        1, 0,
        core.astype(jnp.int32).reshape(1), got, other,
    )
    return out, grad_input, grad_one, grad_two, grad_down, grad_coarse


def solution(mesh):
    whole = jax.sharding.Mesh(mesh.devices.reshape(16, 4, 2), ("gx", "x", "core"))
    fine, coarse = P(None, "gx", GY, None), P("gx", None, GY)
    return jax.shard_map(
        per_device,
        mesh=whole,
        in_specs=(fine, P(), P(), P(), P(), coarse),
        out_specs=(coarse, fine, P(), P(), P(), P()),
        check_vma=False,
    )
```

```python
import jax
import jax.numpy as jnp
from jax import lax
from jax.experimental import pallas as pl
from jax.experimental.pallas import tpu as pltpu
from jax.sharding import PartitionSpec as P

BF = jnp.bfloat16
F32 = jnp.float32
C = 48
CD = 96
CC = 192
Z = 128
GY = ("x", "core")
ALL = ("gx", "x", "core")
SAME_CORE = ("gx", "x")


def dot(a, b):
    return jnp.dot(a, b, preferred_element_type=F32)


def dot_t(a, b):
    return lax.dot_general(a, b, (((1,), (1,)), ((), ())), preferred_element_type=F32)


def sigmoid(v):
    return 0.5 * jnp.tanh(0.5 * v) + 0.5


def from_before(v, segment):
    lane = lax.broadcasted_iota(jnp.int32, v.shape, 1)
    return jnp.where(lane % segment == 0, 0.0, pltpu.roll(v, 1, 1))


def from_after(v, segment):
    lane = lax.broadcasted_iota(jnp.int32, v.shape, 1)
    return jnp.where(lane % segment == segment - 1, 0.0, pltpu.roll(v, Z - 1, 1))


def tap_sum(y, lanes, rows, segment, flipped):
    one, two, three = (y[k * rows : (k + 1) * rows, lanes * Z : (lanes + 1) * Z] for k in range(3))
    if flipped:
        return from_after(one, segment) + two + from_before(three, segment)
    return from_before(one, segment) + two + from_after(three, segment)


def swap_halves(v):
    return pltpu.roll(v.astype(F32), Z // 2, 1)


def low_lanes(shape):
    return lax.broadcasted_iota(jnp.int32, shape, 1) < Z // 2


def put(taps, x, piece, y, count):
    for b in range(3):
        if 0 <= y - b < count:
            at = x * (3 * C) + b * C
            if not isinstance(x, int):
                at = pl.multiple_of(at, 16)
            taps[pl.ds(at, C), (y - b) * Z : (y - b + 1) * Z] = piece


def put_back(taps, x, piece, y, count):
    for b in range(3):
        if 0 <= y - 2 + b < count:
            at = x * (3 * C) + b * C
            if not isinstance(x, int):
                at = pl.multiple_of(at, 16)
            taps[pl.ds(at, C), (y - 2 + b) * Z : (y - 1 + b) * Z] = piece


def put_left(left, x, y, grad):
    lanes = slice(y * Z, (y + 1) * Z)
    wide = grad.astype(F32)
    left[x, :C, lanes] = from_after(wide, Z).astype(BF)
    left[x, C : 2 * C, lanes] = grad
    left[x, 2 * C :, lanes] = from_before(wide, Z).astype(BF)


def fine_kernel(
    flags, feat_l, feat_m, feat_r, one, two, down,
    kept_six, kept_eight, coarse_in,
    w_one, w_two, w_down, taps_one, taps_two, act_v, rows_two, down_all, slope_a, slope_b, sems,
):
    feats = (feat_l, feat_m, feat_r)
    inner = pl.ds(3, 6)
    copies = [
        pltpu.make_async_copy(
            feat_l.at[inner, pl.ds(3 * C, C), :], kept_six.at[pl.ds(12, 6), pl.ds(0, C), :], sems.at[0]
        ),
        pltpu.make_async_copy(
            feat_m.at[inner], kept_six.at[pl.ds(12, 6), pl.ds(C, 4 * C), :], sems.at[1]
        ),
        pltpu.make_async_copy(
            feat_r.at[inner, pl.ds(0, C), :], kept_six.at[pl.ds(12, 6), pl.ds(5 * C, C), :], sems.at[2]
        ),
        pltpu.make_async_copy(
            act_v.at[pl.ds(2, 6)], kept_six.at[pl.ds(0, 6)], sems.at[3]
        ),
        pltpu.make_async_copy(
            slope_a.at[pl.ds(2, 6)], kept_six.at[pl.ds(6, 6)], sems.at[4]
        ),
        pltpu.make_async_copy(slope_b, kept_eight.at[pl.ds(0, 8)], sems.at[5]),
        pltpu.make_async_copy(
            down_all.at[pl.ds(1, 2), :, pl.ds(Z, Z)], kept_eight.at[pl.ds(8, 2)], sems.at[6]
        ),
    ]
    for copy in copies[:3]:
        copy.start()
    for taps, w in ((one, w_one), (two, w_two)):
        for c in range(3):
            w[c * C : (c + 1) * C, :] = grouped(taps, c).astype(BF)
    w_down[...] = jnp.concatenate([down[k].astype(F32) for k in range(8)], axis=1).astype(BF)

    def valid(x, lo, hi):
        ok_l = jnp.where(x < lo, flags[0], 1.0)
        return jnp.where(x >= hi, flags[1], ok_l)

    def valid_y(y, lo, hi):
        if y < lo:
            return flags[2]
        if y >= hi:
            return flags[3]
        return 1.0

    def spread_one(x, carry):
        for y in range(12):
            piece = feats[y // 4][x, (y % 4) * C : (y % 4 + 1) * C, :]
            put(taps_one, x, piece, y, 10)
        return carry

    lax.fori_loop(0, 12, spread_one, 0, unroll=4)

    def step_one(x, carry):
        prod = dot(w_one[...], taps_one[pl.ds(pl.multiple_of(x * 3 * C, 16), 9 * C), :])
        ok_x = valid(x, 3, 7)
        for y in range(10):
            pre = tap_sum(prod, y, C, Z, False)
            sig = sigmoid(pre)
            ok = ok_x * valid_y(y, 3, 7)
            act = (pre * sig * ok).astype(BF)
            put(taps_two, x, act, y, 8)
            if 2 <= y < 8:
                slp = (sig * (1.0 + pre * (1.0 - sig)) * ok).astype(BF)

                act_v[x, (y - 2) * C : (y - 1) * C, :] = act
                slope_a[x, (y - 2) * C : (y - 1) * C, :] = slp
        return carry

    lax.fori_loop(0, 10, step_one, 0, unroll=10)
    copies[3].start()
    copies[4].start()

    row = lax.broadcasted_iota(jnp.int32, (2 * Z, 2 * Z), 0)
    col = lax.broadcasted_iota(jnp.int32, (2 * Z, 2 * Z), 1)
    same = (row // Z) == (col % Z) // (Z // 2)
    select = jnp.where(same & (row % Z == 2 * (col % (Z // 2)) + col // Z), 1.0, 0.0).astype(BF)

    def step_two(x, carry):
        prod = dot(w_two[...], taps_two[pl.ds(pl.multiple_of(x * 3 * C, 16), 9 * C), :])
        ok_x = valid(x, 2, 6)
        for y in range(8):
            pre = tap_sum(prod, y, C, Z, False)
            sig = sigmoid(pre)
            ok = ok_x * valid_y(y, 2, 6)
            act = (pre * sig * ok).astype(BF)
            slope_b[x, y * C : (y + 1) * C, :] = (sig * (1.0 + pre * (1.0 - sig)) * ok).astype(BF)
            pair, b = y // 2, y % 2
            if pair < 3:
                rows_two[(pair * 2 + b) * C : (pair * 2 + b + 1) * C, :Z] = act
            if pair > 0:
                rows_two[((pair - 1) * 2 + b) * C : ((pair - 1) * 2 + b + 1) * C, Z:] = act
        picked = dot(rows_two[...], select).astype(BF)
        a = x % 2
        for pair in range(3):
            for b in range(2):
                for c in range(2):
                    at = pl.multiple_of(a * (4 * C) + (b * 2 + c) * C, 16)
                    down_all[x // 2, pl.ds(at, C), pair * Z : (pair + 1) * Z] = picked[
                        (pair * 2 + b) * C : (pair * 2 + b + 1) * C, c * Z : (c + 1) * Z
                    ]
        return carry

    lax.fori_loop(0, 8, step_two, 0, unroll=8)
    copies[5].start()
    copies[6].start()
    for x in range(4):
        coarse_in[x] = dot(w_down[...], down_all[x]).astype(BF)
    for copy in copies:
        copy.wait()


def coarse_kernel(coarse_in, w_coarse, cot, coarse_out, grad_three):
    total = jnp.zeros((3 * CC, 2 * Z), F32)
    for a in range(3):
        for b in range(3):
            cells = jnp.concatenate(
                [coarse_in[a + x, :, b * Z : (b + 1) * Z] for x in range(2)], axis=1
            )
            total = total + dot(w_coarse[a * 3 + b], cells)
    for x in range(2):
        pre = tap_sum(total, x, CC, Z // 2, False)
        sig = sigmoid(pre)
        coarse_out[x] = (pre * sig).astype(BF)
        grad_three[x] = (cot[x].astype(F32) * (sig * (1.0 + pre * (1.0 - sig)))).astype(BF)


def grouped(taps, c):
    first = lax.broadcasted_iota(jnp.int32, (C, C // 2), 0) < C // 2
    parts = []
    for ab in range(9):
        tap = taps[ab * 3 + c].astype(F32)
        parts += [jnp.where(first, tap, 0.0), jnp.where(first, 0.0, tap)]
    return jnp.concatenate(parts, axis=1)


def back_kernel(one, two, down, coarse, one_out, two_out, down_out, coarse_out,
                w_one_t, w_two_t, w_down_t, w_coarse_t, sems):
    copies = [
        pltpu.make_async_copy(src, dst, sems.at[k])
        for k, (src, dst) in enumerate((
            (w_one_t, one_out), (w_two_t, two_out), (w_down_t, down_out), (w_coarse_t, coarse_out.at[pl.ds(0, 9)])
        ))
    ]
    for taps, out in ((one, w_one_t), (two, w_two_t)):
        for c in range(3):
            turned = grouped(taps, c).T
            out[c * C : (c + 1) * C, :] = jnp.concatenate(
                [
                    turned[ab * C : (ab + 1) * C, :]
                    for ab in (6, 7, 8, 3, 4, 5, 0, 1, 2)
                ],
                axis=1,
            ).astype(BF)
    for ab in range(4):
        w_down_t[ab * C : (ab + 1) * C, :] = jnp.concatenate(
            [down[ab * 2 + c].astype(F32).T for c in range(2)], axis=1
        ).astype(BF)

    def turn(ab, carry):
        for c in range(3):
            w_coarse_t[ab, c * CD : (c + 1) * CD, :] = (
                coarse[ab, c * CC : (c + 1) * CC, :].astype(F32).T.astype(BF)
            )
        return carry

    for copy in copies[:3]:
        copy.start()
    lax.fori_loop(0, 9, turn, 0, unroll=3)
    copies[3].start()
    for copy in copies:
        copy.wait()


def final_kernel(core, got, other, out, out_one, out_two, out_down, wide, small, lined):
    for c in range(2):
        for mine, rows in ((True, got), (False, other)):

            @pl.when((core[0] == c) == mine)
            def _():
                for j in range(64):
                    at = c * 2048 + j * 32
                    wide[at : at + 32, :] = rows[j, :32, :].astype(F32)
                    at = c * 512 + j * 8
                    small[at : at + 8, :] = rows[j, 32:, :].astype(F32)

    for ab in range(9):
        for r in range(144):
            q, s = r // 3, r % 3
            out[ab // 3, ab % 3, :, r * Z : (r + 1) * Z] = wide[
                pl.ds(ab * 432 + s * 48 + q, 3, stride=144), :
            ]

    for base, result in ((0, out_one), (288, out_two)):
        picked = [
            jnp.concatenate(
                [small[pl.ds(base + s * 144 + k, 9, stride=16), :] for s in range(2)], axis=1
            )
            for k in range(16)
        ]
        for ab in range(9):
            line = jnp.concatenate([p[:, ab * 24 : (ab + 1) * 24] for p in picked], axis=1)
            for s in range(3):
                lined[s, :9, :] = line[:, s * Z : (s + 1) * Z]
                for k in range(3):
                    at = k * 384 + s * Z
                    result[ab // 3, ab % 3, :, at : at + Z] = lined[
                        s, pl.ds(k, 3, stride=3), :
                    ]
    picked = [
        jnp.concatenate(
            [small[pl.ds(576 + s * CD + k, 12, stride=8), :] for s in range(3)], axis=1
        )
        for k in range(8)
    ]
    for abc in range(8):
        line = jnp.concatenate([p[:, abc * C : (abc + 1) * C] for p in picked], axis=1)
        for k in range(12):
            out_down[abc // 4, abc // 2 % 2, abc % 2 : abc % 2 + 1, k * 384 : (k + 1) * 384] = line[
                k : k + 1, :
            ]


def coarse_grad_kernel(grad_three, coarse_in, out, shifted, left):
    for x in range(2):
        grad = grad_three[x].astype(F32)
        lanes = slice(x * Z, (x + 1) * Z)
        shifted[x, 0] = from_after(grad, Z // 2)
        shifted[x, 1] = grad
        shifted[x, 2] = from_before(grad, Z // 2)
        for c in range(3):
            for r in range(4):
                left[(c * 4 + r) * 48 : (c * 4 + r + 1) * 48, lanes] = shifted[
                    x, c, pl.ds(r, 48, stride=4), :
                ].astype(BF)
    for a in range(3):
        for b in range(3):
            cells = jnp.concatenate(
                [coarse_in[a + x, :, b * Z : (b + 1) * Z] for x in range(2)], axis=1
            )
            part = dot_t(left[...], cells)
            for c in range(3):
                wide = jnp.concatenate(
                    [part[(c * 4 + r) * 48 : (c * 4 + r + 1) * 48, :] for r in range(4)], axis=1
                ).astype(BF)
                tap = (a * 3 + b) * 3 + c
                for s in range(3):
                    at = (tap * 3 + s) * 48
                    out[at : at + 48, :] = wide[:, s * Z : (s + 1) * Z]
    out[81 * 48 :, :] = jnp.zeros((4096 - 81 * 48, Z), BF)


def backward_kernel(
    g_l, g_m, g_r, coarse_hbm, down_hbm, two_hbm, kept_six, kept_eight,
    mid_out, small,
    w_coarse_t, down_own, w_down_t, slope_two, act_one, w_two_t, slope_one, feat_six,
    halves, spread, mid_one, taps, taps_mid, left, sems,
):
    loads = [
        pltpu.make_async_copy(src, dst, sems.at[k])
        for k, (src, dst) in enumerate((
            (coarse_hbm.at[pl.ds(0, 9)], w_coarse_t), (kept_eight.at[pl.ds(8, 2)], down_own),
            (down_hbm, w_down_t), (kept_eight.at[pl.ds(0, 8)], slope_two),
            (kept_six.at[pl.ds(0, 6)], act_one), (two_hbm, w_two_t),
            (kept_six.at[pl.ds(6, 6)], slope_one), (kept_six.at[pl.ds(12, 6)], feat_six),
        ))
    ]
    for load in loads:
        load.start()
    store = pltpu.make_async_copy(mid_one, mid_out, sems.at[8])
    low = low_lanes((CC, Z))

    def prepare(x, carry):
        p0, p1, p2 = g_l[x], g_m[x], g_r[x]
        s0, s1, s2 = swap_halves(p0), swap_halves(p1), swap_halves(p2)
        halves[0, x, :, :Z] = p1
        halves[0, x, :, Z:] = p2
        halves[1, x, :, :Z] = jnp.where(low, s0, s1).astype(BF)
        halves[1, x, :, Z:] = jnp.where(low, s1, s2).astype(BF)
        halves[2, x, :, :Z] = p0
        halves[2, x, :, Z:] = p1
        return carry

    lax.fori_loop(0, 6, prepare, 0)

    row = lax.broadcasted_iota(jnp.int32, (Z, 4 * Z), 0)
    col = lax.broadcasted_iota(jnp.int32, (Z, 4 * Z), 1)
    same = row // (Z // 2) == col // (2 * Z)
    place = jnp.where(same & (col % Z == 2 * (row % (Z // 2)) + (col // Z) % 2), 1.0, 0.0).astype(BF)
    low_down = low_lanes((CD, Z))

    for load in loads[:4]:
        load.wait()
    grad_down = jnp.zeros((CD, 8 * C), F32)
    for x in range(4):
        total = jnp.zeros((3 * CD, 2 * Z), F32)
        for a in range(3):
            for b in range(3):
                total = total + dot(w_coarse_t[a * 3 + b], halves[b, x + 2 - a])
        back = [tap_sum(total, k, CD, Z // 2, True).astype(BF) for k in range(2)]
        if x == 1 or x == 2:
            own = jnp.where(low_down, swap_halves(back[0]), swap_halves(back[1])).astype(BF)
            grad_down = grad_down + dot_t(own, down_own[x - 1])
        for k in range(2):
            wide = dot(back[k], place).astype(BF)
            for y in range(2):
                for c in range(2):
                    spread[c * CD : (c + 1) * CD, (k * 2 + y) * Z : (k * 2 + y + 1) * Z] = wide[
                        :, (y * 2 + c) * Z : (y * 2 + c + 1) * Z
                    ]
        fine = dot(w_down_t[...], spread[...])
        for a in range(2):
            for b in range(2):
                for y in range(4):
                    rows = slice((2 * y + b) * C, (2 * y + b + 1) * C)
                    part = fine[(a * 2 + b) * C : (a * 2 + b + 1) * C, y * Z : (y + 1) * Z]
                    mid = (part * slope_two[2 * x + a, rows, :].astype(F32)).astype(BF)
                    put_back(taps_mid, 2 * x + a, mid, 2 * y + b, 6)
                    if 0 < x < 3 and 0 < y < 3:
                        put_left(left, 2 * x + a - 2, 2 * y + b - 2, mid)
    for s in range(3):
        small[576 + s * CD : 576 + (s + 1) * CD, :] = grad_down[:, s * Z : (s + 1) * Z].astype(BF)

    small[864:, :] = jnp.zeros((1024 - 864, Z), BF)

    def kernel_grad(field, at):
        for x in range(6):
            for y in range(6):
                put(taps, x, field[x, y * C : (y + 1) * C, :], y, 4)
        part = jnp.zeros((3 * C, 9 * C), F32)
        for x in range(4):
            part = part + dot_t(left[x], taps[x * 3 * C : (x + 3) * 3 * C, :])
        row = lax.broadcasted_iota(jnp.int32, part.shape, 0)
        col = lax.broadcasted_iota(jnp.int32, part.shape, 1)
        part = jnp.where((row % C) // 24 == (col % C) // 24, part, 0.0).astype(BF)
        row = lax.broadcasted_iota(jnp.int32, (432, 256), 0)
        col = lax.broadcasted_iota(jnp.int32, (432, 256), 1)
        fold = jnp.where((row // C == col // 24) & (row % 24 == col % 24), 1.0, 0.0).astype(BF)
        part = dot(part, fold).astype(BF)
        for s in range(2):
            small[at + s * 144 : at + (s + 1) * 144, :] = part[:, s * Z : (s + 1) * Z]

    loads[4].wait()
    kernel_grad(act_one, 288)

    loads[5].wait()
    loads[6].wait()

    def step_two(x, carry):
        prod = dot(w_two_t[...], taps_mid[pl.ds(pl.multiple_of(x * 3 * C, 16), 9 * C), :])
        for y in range(6):
            rows = slice(y * C, (y + 1) * C)
            grad = tap_sum(prod, y, C, Z, True)
            mid = (grad * slope_one[x, rows, :].astype(F32)).astype(BF)
            mid_one[x, rows, :] = mid
        return carry

    lax.fori_loop(0, 6, step_two, 0, unroll=6)

    store.start()
    for x in range(4):
        for y in range(4):
            put_left(left, x, y, mid_one[x + 1, (y + 1) * C : (y + 2) * C, :])
    loads[7].wait()
    kernel_grad(feat_six, 0)
    store.wait()


def input_kernel(mid_one, w_one_t, grad_input, taps):
    for x in range(6):
        for y in range(6):
            put_back(taps, x, mid_one[x, y * C : (y + 1) * C, :], y, 4)
    for x in range(4):
        prod = dot(w_one_t[...], taps[x * 3 * C : (x + 3) * 3 * C, :])
        for y in range(4):
            grad_input[x, y * C : (y + 1) * C, :] = tap_sum(prod, y, C, Z, True).astype(BF)


def call(kernel, outs, scratch, n_smem, flops, *args, far_in=(), far_out=(), limit=20):
    vmem = pl.BlockSpec(memory_space=pltpu.VMEM)
    hbm = pl.BlockSpec(memory_space=pltpu.HBM)
    smem = pl.BlockSpec(memory_space=pltpu.SMEM)
    moved = sum(a.size * a.dtype.itemsize for a in args) + sum(
        o.size * o.dtype.itemsize for o in outs
    )
    return pl.pallas_call(
        kernel,
        out_shape=outs,
        in_specs=[
            smem if k < n_smem else hbm if k in far_in else vmem for k in range(len(args))
        ],
        out_specs=[hbm if k in far_out else vmem for k in range(len(outs))],
        scratch_shapes=scratch,
        compiler_params=pltpu.CompilerParams(vmem_limit_bytes=limit * 1024 * 1024),
        cost_estimate=pl.CostEstimate(flops=flops, bytes_accessed=moved, transcendentals=0),
    )(*args)


def shape(dims, dtype=BF):
    return jax.ShapeDtypeStruct(dims, dtype)


def neighbours(array, axis):
    size = lax.axis_size(axis)
    up = [(i, i + 1) for i in range(size - 1)]
    down = [(j, i) for i, j in up]
    return lax.ppermute(array, axis, up), lax.ppermute(array, axis, down)


def other_core(array):
    return lax.ppermute(array, "core", [(0, 1), (1, 0)])


def pair_sum(parts, core, kept=None):
    half = parts.shape[0] // 2
    keep = lax.dynamic_slice_in_dim(parts if kept is None else kept, core * half, half, 0)
    send = lax.dynamic_slice_in_dim(parts, (1 - core) * half, half, 0)
    both = keep.astype(F32) + other_core(send).astype(F32)
    return both.astype(BF).reshape(64, half // 64, Z)


def per_device(features, conv_one, conv_two, down_weight, coarse_weight, cotangent):
    gx, gy, core = lax.axis_index("gx"), lax.axis_index(GY), lax.axis_index("core")
    last_x, last_y = lax.axis_size("gx") - 1, lax.axis_size(GY) - 1
    flags = jnp.stack([gx > 0, gx < last_x, gy > 0, gy < last_y]).astype(F32)

    feat = jnp.transpose(features, (1, 2, 0, 3)).reshape(4, 4 * C, Z)
    before, after = neighbours(feat, "gx")
    one = conv_one.reshape(27, C, C // 2)
    two = conv_two.reshape(27, C, C // 2)
    w_coarse = coarse_weight.reshape(9, 3 * CC, CD)
    before, after, one, two, w_coarse = lax.optimization_barrier(
        (before, after, one, two, w_coarse)
    )
    feat = jnp.concatenate([before, feat, after], axis=0)
    cot = jnp.transpose(cotangent.reshape(12, 16, 2, Z), (1, 0, 2, 3)).astype(BF)
    feat, cot, down_weight = lax.optimization_barrier((feat, cot, down_weight))
    down = down_weight.reshape(8, CD, C)
    feat_l, feat_r = neighbours(feat, GY)
    cot = lax.all_to_all(cot, "gx", 0, 0, tiled=True)

    kept_six, kept_eight, coarse_in = call(
        fine_kernel,
        [shape((400, 6 * C, Z)), shape((300, 8 * C, Z)), shape((4, CD, 3 * Z))],
        [
            pltpu.VMEM((144, 432), BF), pltpu.VMEM((144, 432), BF), pltpu.VMEM((CD, 8 * C), BF),
            pltpu.VMEM((36 * C, 10 * Z), BF), pltpu.VMEM((30 * C, 8 * Z), BF),
            pltpu.VMEM((10, 6 * C, Z), BF), pltpu.VMEM((6 * C, 2 * Z), BF), pltpu.VMEM((4, 8 * C, 3 * Z), BF),
            pltpu.VMEM((10, 6 * C, Z), BF), pltpu.VMEM((8, 8 * C, Z), BF),
            pltpu.SemaphoreType.DMA((7,)),
        ],
        1, 16_000_000_000,
        flags, feat_l, feat, feat_r, one, two, down, far_out=range(2), limit=40,
    )
    coarse_in, cot = lax.optimization_barrier((coarse_in, cot))
    cot = jnp.transpose(cot.reshape(CC, 2, Z), (1, 0, 2))
    coarse_out, grad_three = call(
        coarse_kernel, [shape((2, CC, Z)), shape((2, CC, Z))], [], 0, 300_000_000,
        coarse_in, w_coarse, cot,
    )

    before, after = neighbours(grad_three, "gx")
    grad_three, one, two, down, w_coarse = lax.optimization_barrier(
        (grad_three, one, two, down, w_coarse)
    )
    backs = [shape((144, 432)), shape((144, 432)), shape((4 * C, 2 * CD)), shape((200, 3 * CD, CC))]
    w_one_t, w_two_t, w_down_t, w_coarse_t = call(
        back_kernel, backs,
        [pltpu.VMEM(w.shape, BF) for w in backs[:3]]
        + [pltpu.VMEM((9, 3 * CD, CC), BF), pltpu.SemaphoreType.DMA((4,))], 0, 0,
        one, two, down, w_coarse, far_out=range(4), limit=40,
    )
    before, after, w_one_t, w_two_t, w_down_t, w_coarse_t = lax.optimization_barrier(
        (before, after, w_one_t, w_two_t, w_down_t, w_coarse_t)
    )
    wide = jnp.concatenate([before, grad_three, after], axis=0)
    g_l, g_r = neighbours(wide, GY)
    wide, grad_own = lax.optimization_barrier((wide, grad_three))
    (coarse_part,) = call(
        coarse_grad_kernel,
        [shape((4096, Z))],
        [pltpu.VMEM((2, 3, CC, Z), F32), pltpu.VMEM((3 * CC, 2 * Z), BF)],
        0, 500_000_000,
        grad_own, coarse_in,
    )
    g_l, g_r, kept = lax.optimization_barrier((g_l, g_r, coarse_part))
    coarse_mine = pair_sum(coarse_part, core, kept)
    slots = jnp.transpose(coarse_out.reshape(2, 16, 12, Z), (1, 0, 2, 3)).reshape(16, 1, 24, Z)
    there = lax.broadcasted_iota(jnp.int32, (16, 4, 24, Z), 1) == lax.axis_index("x")
    slots = jnp.where(there, slots, jnp.zeros((), BF)).reshape(64, 24, Z)

    mid_one, small = call(
        backward_kernel,
        [shape((6, 6 * C, Z)), shape((1024, Z))],
        [
            pltpu.VMEM((9, 3 * CD, CC), BF), pltpu.VMEM((2, 8 * C, Z), BF),
            pltpu.VMEM((4 * C, 2 * CD), BF), pltpu.VMEM((8, 8 * C, Z), BF),
            pltpu.VMEM((6, 6 * C, Z), BF), pltpu.VMEM((144, 432), BF),
            pltpu.VMEM((6, 6 * C, Z), BF), pltpu.VMEM((6, 6 * C, Z), BF),
            pltpu.VMEM((3, 6, CC, 2 * Z), BF), pltpu.VMEM((2 * CD, 4 * Z), BF),
            pltpu.VMEM((6, 6 * C, Z), BF), pltpu.VMEM((18 * C, 4 * Z), BF),
            pltpu.VMEM((24 * C, 6 * Z), BF), pltpu.VMEM((4, 3 * C, 4 * Z), BF),
            pltpu.SemaphoreType.DMA((9,)),
        ],
        0, 12_000_000_000,
        g_l, wide, g_r, w_coarse_t, w_down_t, w_two_t, kept_six, kept_eight,
        far_in=range(3, 8), far_out=(0,), limit=40,
    )
    small, coarse_mine, slots = lax.optimization_barrier((small, coarse_mine, slots))
    parts = jnp.concatenate([coarse_mine, pair_sum(small, core), slots], axis=1)
    parts = lax.all_to_all(parts, SAME_CORE, 0, 0, tiled=True)
    out = lax.dynamic_index_in_dim(
        parts[:, 40:].reshape(16, 4, 24, Z), lax.axis_index("x"), 1, keepdims=False
    )
    mine = jnp.sum(parts[:, :40].astype(F32), axis=0).astype(BF)
    (grad_input,) = call(
        input_kernel, [shape((4, 4 * C, Z))], [pltpu.VMEM((18 * C, 4 * Z), BF)], 0, 1_000_000_000,
        mid_one, w_one_t,
    )
    got = lax.all_to_all(
        jnp.broadcast_to(mine[None], (64,) + mine.shape), SAME_CORE, 0, 0, tiled=True
    )
    other = other_core(got)
    out = jnp.transpose(out.reshape(32, 12, Z), (1, 0, 2))
    grad_input = jnp.transpose(grad_input.reshape(4, 4, C, Z), (2, 0, 1, 3))

    grad_coarse, grad_one, grad_two, grad_down = call(
        final_kernel,
        [
            shape((3, 3, 3, CC * CD), F32), shape((3, 3, 3, C * 24), F32),
            shape((3, 3, 3, C * 24), F32), shape((2, 2, 2, CD * C), F32),
        ],
        [pltpu.VMEM((4096, Z), F32), pltpu.VMEM((1024, Z), F32), pltpu.VMEM((3, 16, Z), F32)],
        1, 0,
        core.astype(jnp.int32).reshape(1), got, other,
    )
    return out, grad_input, grad_one, grad_two, grad_down, grad_coarse


def solution(mesh):
    whole = jax.sharding.Mesh(mesh.devices.reshape(16, 4, 2), ("gx", "x", "core"))
    fine, coarse = P(None, "gx", GY, None), P("gx", None, GY)
    return jax.shard_map(
        per_device,
        mesh=whole,
        in_specs=(fine, P(), P(), P(), P(), coarse),
        out_specs=(coarse, fine, P(), P(), P(), P()),
        check_vma=False,
    )
```
